256 devices in a mesh: side: 2 (over core), group: 4 (over x), dev: 32 (over y, z).
Axes of the slice: x: 4, y: 4, z: 8, core: 2. Of those that a mesh axis runs over, the one named last changes fastest.
Arguments:
- embeds: bfloat16 [2, 1536, 256, 256], P('side', ('group', 'dev')), may hold values from -0.5 to 0.5
- log_weights: float32 [2, 1536, 256], P('side', ('group', 'dev')), may hold values from -4 to 4
- listing: int32 [2, 7680, 2], P('side', ('group', 'dev')), may hold values from 0 to 1535, as said below
Outputs:
- potential: float32 [2, 1536, 256], P('side', ('group', 'dev'))
The draws below stay inside these ranges and needn't reach their ends.
Inputs may be any that keep to these rules, and one draw needn't show every extreme that they name: Block b of a side lies on device b // 12 of that side (group+dev order). Device e of side s holds in listing[s] exactly the 60 pairs whose side-s block lies on it; listing[1] holds the pairs of listing[0] with the two ids swapped, each once. Every block of either side is in 2 or 8 listed pairs. The pairs between the blocks of one device and the blocks of one device of the other side number at most 1, and every device has such a partner device with exactly 1.
All inputs are finite; a program needn't handle non-finite values.
Results may differ from the reference program's by a relative error of at most 0.0003.
Values may be sent and summed in bfloat16 or wider, within the bound.
A program may use at most 128 MiB of HBM per device.

```python
import jax
import jax.numpy as jnp
import numpy as np
from jax import lax

D = 256
BLK = 256
BLK_DEV = 12
DEG_LO = 2
MOST = 8
ITERS = 3
HALF_DEVS = 128
NB = 1536
PAIRS_DEV = 60
NPAIRS = 7680


def draw_embeds(key, part):
    key = jax.random.fold_in(key, 5)
    shape = (2, NB, BLK, D)
    center_key, first_key = jax.random.split(key, 2)
    centers = jax.random.normal(center_key, (2, NB, 1, D), jnp.float32) * 0.06
    values = jnp.clip(centers + jax.random.normal(first_key, shape, jnp.float32) * 0.08, -0.5, 0.5)
    return values.astype(jnp.bfloat16)


def local_blocks(key, dev_count):
    first_key, second_key = jax.random.split(key)
    slot_perm = jax.vmap(lambda sub_key: jax.random.permutation(sub_key, PAIRS_DEV))(jax.random.split(first_key, dev_count))
    block_perm = jax.vmap(lambda sub_key: jax.random.permutation(sub_key, BLK_DEV))(jax.random.split(second_key, dev_count))
    degrees = np.where(np.arange(BLK_DEV) % 2 == 0, DEG_LO, MOST)
    base_list = jnp.asarray(np.repeat(np.arange(BLK_DEV), degrees), jnp.int32)
    return jnp.take_along_axis(block_perm.astype(jnp.int32), base_list[slot_perm], axis=1)


def draw_listing(key, part):
    key = jax.random.fold_in(key, 9)
    key_list = jax.random.split(key, 4)
    dev_count = HALF_DEVS
    first_perm = jax.random.permutation(key_list[0], dev_count).astype(jnp.int32)
    second_perm = jax.random.permutation(key_list[1], dev_count).astype(jnp.int32)
    dev_index = jnp.arange(dev_count, dtype=jnp.int32)
    first_inv = jnp.zeros(dev_count, jnp.int32).at[first_perm].set(dev_index)
    second_inv = jnp.zeros(dev_count, jnp.int32).at[second_perm].set(dev_index)
    src_local = local_blocks(key_list[2], dev_count)
    tgt_local = local_blocks(key_list[3], dev_count)
    rounds = jnp.arange(PAIRS_DEV, dtype=jnp.int32)
    target_dev = second_perm[(first_perm[:, None] + rounds[None, :]) % dev_count]
    source_dev = first_inv[(second_inv[:, None] - rounds[None, :]) % dev_count]
    src_block = dev_index[:, None] * BLK_DEV + src_local
    tgt_of_src = target_dev * BLK_DEV + tgt_local[target_dev, rounds[None, :]]
    side_first = jnp.stack([src_block, tgt_of_src], axis=-1).reshape(NPAIRS, 2)
    tgt_block = dev_index[:, None] * BLK_DEV + tgt_local
    src_of_tgt = source_dev * BLK_DEV + src_local[source_dev, rounds[None, :]]
    side_second = jnp.stack([tgt_block, src_of_tgt], axis=-1).reshape(NPAIRS, 2)
    return jnp.stack([side_first, side_second]).astype(jnp.int32)


def block_scale(stream_key, extent, cuts, low, high):
    def one(dim, parts):
        heights = jax.random.uniform(jax.random.fold_in(jax.random.fold_in(stream_key, 6), dim), (parts,), jnp.float32, low / len(cuts), high / len(cuts))
        return jnp.repeat(jnp.exp(heights), extent[dim] // parts).reshape((-1,) + (1,) * (len(extent) - dim - 1))

    loudness = one(*cuts[0])
    for cut in cuts[1:]:
        loudness = loudness * one(*cut)
    return loudness


def gaussian(stream_key, shape, deviation, reach, shards=(), kind=jnp.bfloat16):
    array = deviation * jax.random.normal(stream_key, shape, jnp.float32)
    if shards:
        array = array * block_scale(stream_key, shape, shards, -0.22, 0.18)
    return jnp.clip(array, -reach, reach).astype(kind)


def setup_inputs(seed: int = 0) -> dict:
    key_of = jax.random.split(jax.random.key(seed), 4)
    return {
        "embeds": draw_embeds(jax.random.fold_in(key_of[3], 71), 0),
        "log_weights": gaussian(key_of[1], (2, NB, BLK), 1.0, 4.0, ((0, 2), (1, 128)), jnp.float32),
        "listing": draw_listing(jax.random.fold_in(key_of[3], 71), 0),
    }


entropic_blur = 0.1


def pair_terms(src_emb, tgt_emb, src_sq, tgt_sq, src_shift, tgt_shift, group_pairs):
    src_ids = group_pairs[:, 0]
    tgt_ids = group_pairs[:, 1]
    src_rows = src_emb[src_ids].astype(jnp.float32)
    tgt_rows = tgt_emb[tgt_ids].astype(jnp.float32)
    cross_term = jnp.einsum("gid,gjd->gij", src_rows, tgt_rows)
    pair_cost = src_sq[src_ids][:, :, None] + tgt_sq[tgt_ids][:, None, :] - 2.0 * cross_term
    scaled = pair_cost / entropic_blur
    row_score = tgt_shift[tgt_ids][:, None, :] - scaled
    row_top = jnp.max(row_score, axis=2)
    row_total = jnp.sum(jnp.exp(row_score - row_top[:, :, None]), axis=2)
    col_score = src_shift[src_ids][:, :, None] - scaled
    col_top = jnp.max(col_score, axis=1)
    col_total = jnp.sum(jnp.exp(col_score - col_top[:, None, :]), axis=1)
    return row_top, row_total, col_top, col_total


def combine(tops, totals, seg_ids, seg_count):
    best = jax.ops.segment_max(tops, seg_ids, num_segments=seg_count)
    weighted = jax.ops.segment_sum(totals * jnp.exp(tops - best[seg_ids]), seg_ids, num_segments=seg_count)
    return best + jnp.log(weighted)


def reference(embeds, log_weights, listing):
    pair_table = listing[0].astype(jnp.int32)
    block_count = embeds.shape[1]
    row_count = embeds.shape[2]
    src_emb = embeds[0]
    tgt_emb = embeds[1]
    src_sq = jnp.sum(jnp.square(src_emb.astype(jnp.float32)), axis=2)
    tgt_sq = jnp.sum(jnp.square(tgt_emb.astype(jnp.float32)), axis=2)
    grouped = pair_table.reshape(-1, 10, 2)
    pair_total = pair_table.shape[0]
    potential = jnp.zeros(log_weights.shape, jnp.float32)
    for iteration in range(ITERS):
        shifted = potential + log_weights

        def run_group(group_pairs):
            return pair_terms(src_emb, tgt_emb, src_sq, tgt_sq, shifted[0], shifted[1], group_pairs)

        row_top, row_total, col_top, col_total = lax.map(run_group, grouped)
        row_top = row_top.reshape(pair_total, row_count)
        row_total = row_total.reshape(pair_total, row_count)
        col_top = col_top.reshape(pair_total, row_count)
        col_total = col_total.reshape(pair_total, row_count)
        src_new = -combine(row_top, row_total, pair_table[:, 0], block_count)
        tgt_new = -combine(col_top, col_total, pair_table[:, 1], block_count)
        potential = 0.5 * (potential + jnp.stack([src_new, tgt_new]))
    return potential
```

```python
import functools
import math

import jax
import jax.numpy as jnp
from jax import lax
from jax.experimental import pallas as pl
from jax.experimental.pallas import tpu as pltpu
from jax.sharding import PartitionSpec as P

MESH = pl.DeviceIdType.MESH
ITERS = 3
NX, NY, NZ = 4, 4, 8
LOG2E = math.log2(math.e)
LN2 = math.log(2.0)
INV_BLUR = 10.0
SCALE = 2.0 * INV_BLUR * LOG2E
EMPTY = -1e30
VMEM_CAP = 48 * 1024 * 1024


def where(pred, a, b):
    return jnp.where(pred, a, b)


class Place:
    def __init__(self):
        self.k = lax.axis_index("side")
        self.x = lax.axis_index("group")
        dev = lax.axis_index("dev")
        self.y = dev // NZ
        self.z = dev % NZ
        self.kq = (self.x + self.y) % 2
        self.own_slot = self.y * 2 + self.x // 2

    def dev(self, k, x, y, z):
        return (k, x, y * NZ + z)

    def owner(self, j):
        if j < 8:
            return self.dev(jnp.int32(0), self.x, self.y, jnp.int32(j)), jnp.logical_and(self.k == 0, self.z == j)
        d = j - 8
        y0 = d // 2
        x0 = 2 * (d % 2) + (y0 + self.k) % 2
        me = jnp.logical_and(self.k == 1, jnp.logical_and(self.x == x0, self.y == y0))
        return self.dev(jnp.int32(1), x0, jnp.int32(y0), self.z), me

    def meeter(self, j):
        src = self.k == 0
        kk = where(src, j % 2, self.kq)
        xx = where(src, self.x, j % 4)
        yy = where(src, self.y, j // 4)
        zz = where(src, j // 2, self.z)
        me = jnp.logical_and(
            jnp.logical_and(kk == self.k, xx == self.x), jnp.logical_and(yy == self.y, zz == self.z)
        )
        return self.dev(kk, xx, yy, zz), me

    def peers(self):
        return 16 - where(jnp.logical_or(self.k == 0, self.kq == 1), 1, 0)

    def level_slot(self):
        return where(self.k == 0, self.z, 8 + self.own_slot)

    def meet_slot(self, j):
        return self.z * 2 + self.k if j < 8 else self.y * 4 + self.x


def remote(src, dst, send_sem, recv_sem, device):
    return pltpu.make_async_remote_copy(
        src_ref=src, dst_ref=dst, send_sem=send_sem, recv_sem=recv_sem, device_id=device, device_id_type=MESH
    )


def spread_start(pc, level, table, send_sem, recv_sem):
    slot = pc.level_slot()
    for j in range(16):
        device, me = pc.meeter(j)

        @pl.when(jnp.logical_not(me))
        def _():
            remote(level, table.at[slot], send_sem.at[j], recv_sem.at[slot], device).start()

        @pl.when(me)
        def _():
            table[slot] = level[...]


def spread_wait(pc, level, table, send_sem, recv_sem):
    for j in range(16):
        device, me = pc.meeter(j)
        owner, mine = pc.owner(j)

        @pl.when(jnp.logical_not(mine))
        def _():
            remote(level, table.at[j], send_sem.at[j], recv_sem.at[j], owner).wait_recv()

    for j in range(16):
        device, me = pc.meeter(j)

        @pl.when(jnp.logical_not(me))
        def _():
            remote(level, table.at[j], send_sem.at[j], recv_sem.at[j], device).wait_send()


def signal(sem, device):
    pl.semaphore_signal(sem, inc=1, device_id=device, device_id_type=MESH)


def gather_kernel(
    emb, level, src_out, tgt_out, level_out, list_out,
    table, local_sem, own_sem, z_send, z_recv, sib_send, sib_recv,
    first_send, first_recv, next_send, next_recv, relay_send, relay_recv, lv_send, lv_recv,
):
    pc = Place()
    k, x, y, z = pc.k, pc.x, pc.y, pc.z
    sibling = pc.dev(1 - k, x, y, z)
    zdev = [pc.dev(k, x, y, (z + 1) % NZ), pc.dev(k, x, y, (z + NZ - 1) % NZ)]
    xdev = [pc.dev(k, (x + 1) % NX, y, z), pc.dev(k, (x + NX - 1) % NX, y, z)]
    ydev = [pc.dev(k, x, (y + 1) % NY, z), pc.dev(k, x, (y + NY - 1) % NY, z)]

    barrier = pltpu.get_barrier_semaphore()
    for device in [sibling] + zdev + xdev + ydev:
        signal(barrier, device)
    for j in range(16):
        device, mine = pc.owner(j)

        @pl.when(jnp.logical_not(mine))
        def _():
            signal(barrier, device)

    pl.semaphore_wait(barrier, 7 + pc.peers())

    native = k == pc.kq

    def src_at(h, z0, s):
        return src_out.at[h, z0, pl.ds(3 * s, 3)]

    def tgt_at(f, line, o, s):
        return tgt_out.at[f, line, o, pl.ds(3 * s, 3)]

    line_of = [y, x]
    spot_of = [x, y]
    spread_dev = [xdev, ydev]
    onward_dev = [ydev, xdev]

    @pl.when(k == 0)
    def _():
        for h in (1, 0):
            for s in range(2):
                part = emb.at[pl.ds(6 * h + 3 * s, 3)]
                remote(part, src_at(h, z, s), own_sem.at[0, h, s], own_sem.at[1, h, s], sibling).start()
        for h in range(2):
            for s in range(2):
                part = emb.at[pl.ds(6 * h + 3 * s, 3)]
                pltpu.make_async_copy(part, src_at(h, z, s), local_sem.at[h, s]).start()

    @pl.when(jnp.logical_and(k == 1, pc.kq == 1))
    def _():
        for f in range(2):
            for s in range(2):
                part = emb.at[pl.ds(6 * f + 3 * s, 3)]
                pltpu.make_async_copy(part, tgt_at(f, line_of[f], spot_of[f] // 2, s), local_sem.at[f, s]).start()

    @pl.when(jnp.logical_and(k == 1, pc.kq == 0))
    def _():
        for f in range(2):
            for s in range(2):
                part = emb.at[pl.ds(6 * f + 3 * s, 3)]
                remote(
                    part, tgt_at(f, line_of[f], spot_of[f] // 2, s), own_sem.at[0, f, s], own_sem.at[1, f, s], sibling
                ).start()

    spread_start(pc, level, table, lv_send, lv_recv)

    def z_copy(way, r, s):
        z0 = (z - r + NZ) % NZ if way == 0 else (z + r) % NZ
        part = src_out.at[k, z0, pl.ds(3 * s, 3)]
        return remote(part, part, z_send.at[way, r, s], z_recv.at[way, r, s], zdev[way])

    def z_landed(way, r, s):
        z0 = (z - r - 1 + NZ) % NZ if way == 0 else (z + r + 1) % NZ
        part = src_out.at[k, z0, pl.ds(3 * s, 3)]
        return remote(part, part, z_send.at[way, r, s], z_recv.at[way, r, s], zdev[way])

    def sib_copy(way, r, s):
        z0 = (z - r - 1 + NZ) % NZ if way == 0 else (z + r + 1) % NZ
        part = src_out.at[k, z0, pl.ds(3 * s, 3)]
        return remote(part, part, sib_send.at[way, r, s], sib_recv.at[way, r, s], sibling)

    def sib_landed(way, r, s):
        z0 = (z - r - 1 + NZ) % NZ if way == 0 else (z + r + 1) % NZ
        part = src_out.at[1 - k, z0, pl.ds(3 * s, 3)]
        return remote(part, part, sib_send.at[way, r, s], sib_recv.at[way, r, s], sibling)

    def z_subs(way, r):
        return (0, 1) if r < 3 else (way,)

    for s in range(2):
        @pl.when(k == 0)
        def _():
            part = emb.at[pl.ds(3 * s, 3)]
            pltpu.make_async_copy(part, src_at(0, z, s), local_sem.at[0, s]).wait()

        @pl.when(k == 1)
        def _():
            part = src_at(1, z, s)
            remote(part, part, own_sem.at[0, 1, s], own_sem.at[1, 1, s], sibling).wait_recv()

        for way in range(2):
            z_copy(way, 0, s).start()

    def first_copy(f, way, o, s):
        part = tgt_at(f, line_of[f], o, s)
        return remote(part, part, first_send.at[f, way, s], first_recv.at[f, way, s], spread_dev[f][way])

    def next_copy(f, way, o, s):
        part = tgt_at(f, line_of[f], o, s)
        return remote(part, part, next_send.at[f, way, o, s], next_recv.at[f, way, o, s], onward_dev[f][way])

    def from_line(f, way):
        n = line_of[f]
        return (n + 3) % 4 if way == 0 else (n + 1) % 4

    def next_landed(f, way, o, s):
        part = tgt_at(f, from_line(f, way), o, s)
        return remote(part, part, next_send.at[f, way, o, s], next_recv.at[f, way, o, s], onward_dev[f][way])

    def relay_copy(f, way, o):
        part = tgt_at(f, from_line(f, way), o, way)
        return remote(part, part, relay_send.at[f, way, o], relay_recv.at[f, way, o], onward_dev[f][way])

    def relay_landed(f, way, o):
        part = tgt_at(f, (line_of[f] + 2) % 4, o, way)
        return remote(part, part, relay_send.at[f, way, o], relay_recv.at[f, way, o], onward_dev[f][way])

    home = [spot_of[f] // 2 for f in range(2)]
    near = [[((spot_of[f] + 3) % 4) // 2, ((spot_of[f] + 1) % 4) // 2] for f in range(2)]

    @pl.when(native)
    def _():
        for s in range(2):
            for f in range(2):
                part = tgt_at(f, line_of[f], home[f], s)

                @pl.when(k == 1)
                def _():
                    pltpu.make_async_copy(emb.at[pl.ds(6 * f + 3 * s, 3)], part, local_sem.at[f, s]).wait()

                @pl.when(k == 0)
                def _():
                    remote(part, part, own_sem.at[0, f, s], own_sem.at[1, f, s], sibling).wait_recv()

                for way in range(2):
                    first_copy(f, way, home[f], s).start()
        for s in range(2):
            for f in range(2):
                for way in range(2):
                    next_copy(f, way, home[f], s).start()

    def z_forward(r):
        for s in range(2):
            for way in range(2):
                if s in z_subs(way, r):
                    z_landed(way, r, s).wait_recv()
                    if r < 3 and s in z_subs(way, r + 1):
                        z_copy(way, r + 1, s).start()
                    sib_copy(way, r, s).start()

    z_forward(0)

    @pl.when(jnp.logical_not(native))
    def _():
        for s in range(2):
            for f in range(2):
                for way in range(2):
                    o = near[f][way]
                    first_copy(f, way, o, s).wait_recv()
                    if s == way:
                        first_copy(f, way, o, s).start()
                    for w in range(2):
                        next_copy(f, w, o, s).start()

    z_forward(1)

    @pl.when(native)
    def _():
        for f in range(2):
            for way in range(2):
                o = 1 - home[f]
                first_copy(f, way, o, way).wait_recv()
                for w in range(2):
                    next_copy(f, w, o, way).start()

    def onward(nth):
        for s in range(2):
            for f in range(2):
                o = home[f] if nth == 0 else 1 - home[f]
                for way in range(2):
                    next_landed(f, way, o, s).wait_recv()
                    if s == way:
                        relay_copy(f, way, o).start()

    onward(0)
    z_forward(2)
    onward(1)
    z_forward(3)

    spread_wait(pc, level, table, lv_send, lv_recv)
    level_out[...] = table[...]
    codes = table[0:8, 12, 0:128]
    low = ((z * 2 + k) * 2048).astype(jnp.float32)
    mine = jnp.logical_and(codes >= low, codes < low + 2048.0)
    hit = jnp.where(mine, 1.0, 0.0)
    row_id = lax.broadcasted_iota(jnp.int32, (128, 128), 0)
    col_id = lax.broadcasted_iota(jnp.int32, (128, 128), 1)
    upper = jnp.where(row_id < col_id, 1.0, 0.0)
    within = jnp.dot(hit, upper, preferred_element_type=jnp.float32)
    totals = jnp.broadcast_to(jnp.sum(hit, axis=1, keepdims=True), (8, 128))
    below = jnp.where(
        lax.broadcasted_iota(jnp.int32, (8, 8), 1) < lax.broadcasted_iota(jnp.int32, (8, 8), 0), 1.0, 0.0
    )
    before = jnp.dot(below, totals, preferred_element_type=jnp.float32, precision=lax.Precision.HIGHEST)
    rank = jnp.where(mine, within + before, -1.0)
    packed = codes - low + 2048.0 * lax.broadcasted_iota(jnp.int32, (8, 128), 0).astype(jnp.float32)
    want = row_id.astype(jnp.float32)
    picked = jnp.zeros((128, 128), jnp.float32)
    for r in range(8):
        picked = picked + jnp.where(want == rank[r : r + 1, :], packed[r : r + 1, :], 0.0)
    entries = jnp.broadcast_to(jnp.sum(picked, axis=1, keepdims=True), (128, 128))
    line = jnp.sum(jnp.where(row_id == col_id, entries, 0.0), axis=0, keepdims=True)
    count = jnp.broadcast_to(jnp.sum(totals[:, 0:1], axis=0, keepdims=True), (1, 128))
    list_out[...] = jnp.concatenate([line, count, jnp.zeros((6, 128), jnp.float32)], axis=0).astype(jnp.int32)

    for f in range(2):
        for way in range(2):
            for o in range(2):
                relay_landed(f, way, o).wait_recv()
    for r in range(4):
        for way in range(2):
            for s in z_subs(way, r):
                sib_landed(way, r, s).wait_recv()

    @pl.when(k == 1)
    def _():
        for s in range(2):
            part = src_at(0, z, s)
            remote(part, part, own_sem.at[0, 0, s], own_sem.at[1, 0, s], sibling).wait_recv()

    @pl.when(k == 0)
    def _():
        for s in range(2):
            part = emb.at[pl.ds(6 + 3 * s, 3)]
            pltpu.make_async_copy(part, src_at(1, z, s), local_sem.at[1, s]).wait()
        for h in range(2):
            for s in range(2):
                part = emb.at[pl.ds(6 * h + 3 * s, 3)]
                remote(part, src_at(h, z, s), own_sem.at[0, h, s], own_sem.at[1, h, s], sibling).wait_send()

    @pl.when(jnp.logical_and(k == 1, pc.kq == 0))
    def _():
        for f in range(2):
            for s in range(2):
                part = emb.at[pl.ds(6 * f + 3 * s, 3)]
                remote(
                    part, tgt_at(f, line_of[f], home[f], s), own_sem.at[0, f, s], own_sem.at[1, f, s], sibling
                ).wait_send()

    for r in range(4):
        for way in range(2):
            for s in z_subs(way, r):
                z_copy(way, r, s).wait_send()
                sib_copy(way, r, s).wait_send()
    for f in range(2):
        for way in range(2):
            for s in range(2):
                @pl.when(native)
                def _():
                    first_copy(f, way, home[f], s).wait_send()

            @pl.when(jnp.logical_not(native))
            def _():
                first_copy(f, way, near[f][way], way).wait_send()

            for o in range(2):
                relay_copy(f, way, o).wait_send()
                for s in range(2):
                    next_copy(f, way, o, s).wait_send()


def gather(emb, level):
    DMA = pltpu.SemaphoreType.DMA
    any_spec = pl.BlockSpec(memory_space=pl.ANY)
    vmem = pl.BlockSpec(memory_space=pltpu.VMEM)
    return pl.pallas_call(
        gather_kernel,
        out_shape=(
            jax.ShapeDtypeStruct((2, 8, 6, 256, 256), jnp.bfloat16),
            jax.ShapeDtypeStruct((2, 4, 2, 6, 256, 256), jnp.bfloat16),
            jax.ShapeDtypeStruct((16, 16, 256), jnp.float32),
            jax.ShapeDtypeStruct((8, 128), jnp.int32),
        ),
        in_specs=[any_spec, vmem],
        out_specs=(any_spec, any_spec, vmem, vmem),
        scratch_shapes=[
            pltpu.VMEM((16, 16, 256), jnp.float32),
            DMA((2, 2)),
            DMA((2, 2, 2)),
            DMA((2, 4, 2)),
            DMA((2, 4, 2)),
            DMA((2, 4, 2)),
            DMA((2, 4, 2)),
            DMA((2, 2, 2)),
            DMA((2, 2, 2)),
            DMA((2, 2, 2, 2)),
            DMA((2, 2, 2, 2)),
            DMA((2, 2, 2)),
            DMA((2, 2, 2)),
            DMA((16,)),
            DMA((16,)),
        ],
        compiler_params=pltpu.CompilerParams(collective_id=0, has_side_effects=True, vmem_limit_bytes=VMEM_CAP),
        name="gather_blocks",
    )(emb, level)


def pair_kernel(pairs, level, src, tgt, part_out, xbuf, ybuf, turned, top, total, sems):
    k = lax.axis_index("side")

    def fetch(p, slot):
        code = pairs[0, p]
        bs = code // 128
        bt = code % 128
        sz = bs // 16
        sb = bs % 16
        d = bt // 16
        tb = bt % 16
        y0 = d // 2
        x0 = 2 * (d % 2) + (y0 + k) % 2
        f = tb // 6
        line = where(f == 0, y0, x0)
        o = where(f == 0, x0, y0) // 2
        return (
            pltpu.make_async_copy(src.at[sb // 6, sz, sb % 6], xbuf.at[slot], sems.at[0, slot]),
            pltpu.make_async_copy(tgt.at[f, line, o, tb % 6], ybuf.at[slot], sems.at[1, slot]),
        )

    count = pairs[1, 0]

    @pl.when(count > 0)
    def _():
        for copy in fetch(0, 0):
            copy.start()

    for g in range(2):
        rows = level[8 * g : 8 * g + 8].reshape(128, 256)
        turned[g] = rows.T
    top[...] = jnp.full(top.shape, EMPTY, jnp.float32)
    total[...] = jnp.zeros(total.shape, jnp.float32)
    lane = lax.broadcasted_iota(jnp.int32, (256, 128), 1)
    contract = (((1,), (1,)), ((), ()))

    def reduce_to(a, b, g_from, index_from, g_to, index_to):
        bias = jnp.sum(jnp.where(lane == index_from, turned[g_from], 0.0), axis=1, keepdims=True)
        score = lax.dot_general(a, b, contract, preferred_element_type=jnp.float32) * SCALE + bias
        peak = jnp.max(score, axis=0, keepdims=True)
        mass = jnp.sum(jnp.exp2(score - peak), axis=0, keepdims=True)
        old_peak = top[g_to, pl.ds(index_to, 1), :]
        old_mass = total[g_to, pl.ds(index_to, 1), :]
        new_peak = jnp.maximum(old_peak, peak)
        top[g_to, pl.ds(index_to, 1), :] = new_peak
        total[g_to, pl.ds(index_to, 1), :] = old_mass * jnp.exp2(old_peak - new_peak) + mass * jnp.exp2(peak - new_peak)

    def body(p, carry):
        slot = p % 2

        @pl.when(p + 1 < count)
        def _():
            for copy in fetch(p + 1, 1 - slot):
                copy.start()

        for copy in fetch(p, slot):
            copy.wait()
        code = pairs[0, p]
        bs = code // 128
        bt = code % 128
        xs = xbuf[slot]
        ys = ybuf[slot]
        reduce_to(xs, ys, 0, bs, 1, bt)
        reduce_to(ys, xs, 1, bt, 0, bs)
        return carry

    lax.fori_loop(0, count, body, 0)
    for g in range(2):
        mass = total[g]
        value = jnp.where(mass > 0.0, top[g] + jnp.log2(jnp.maximum(mass, 1e-37)), EMPTY)
        part_out[8 * g : 8 * g + 8] = value.reshape(8, 16, 256)


def pair_pass(pairs, level, src, tgt):
    any_spec = pl.BlockSpec(memory_space=pl.ANY)
    vmem = pl.BlockSpec(memory_space=pltpu.VMEM)
    return pl.pallas_call(
        pair_kernel,
        out_shape=jax.ShapeDtypeStruct((16, 16, 256), jnp.float32),
        in_specs=[pl.BlockSpec(memory_space=pltpu.SMEM), vmem, any_spec, any_spec],
        out_specs=vmem,
        scratch_shapes=[
            pltpu.VMEM((2, 256, 256), jnp.bfloat16),
            pltpu.VMEM((2, 256, 256), jnp.bfloat16),
            pltpu.VMEM((2, 256, 128), jnp.float32),
            pltpu.VMEM((2, 128, 256), jnp.float32),
            pltpu.VMEM((2, 128, 256), jnp.float32),
            pltpu.SemaphoreType.DMA((2, 2)),
        ],
        compiler_params=pltpu.CompilerParams(vmem_limit_bytes=VMEM_CAP),
        name="pair_sums",
    )(pairs, level, src, tgt)


def exchange_kernel(last, part, pot, weight, norm, *rest):
    if last:
        pot_out, gathered, send1, recv1 = rest
    else:
        pot_out, level_out, gathered, level, table, send1, recv1, send2, recv2 = rest
    pc = Place()
    barrier = pltpu.get_barrier_semaphore()
    for j in range(16):
        device, me = pc.meeter(j)

        @pl.when(jnp.logical_not(me))
        def _():
            signal(barrier, device)

    pl.semaphore_wait(barrier, pc.peers())

    for j in range(16):
        device, mine = pc.owner(j)
        slot = pc.meet_slot(j)

        @pl.when(jnp.logical_not(mine))
        def _():
            remote(part.at[j], gathered.at[slot], send1.at[j], recv1.at[slot], device).start()

        @pl.when(mine)
        def _():
            gathered[slot] = part[j]

    for j in range(16):
        device, me = pc.meeter(j)

        @pl.when(jnp.logical_not(me))
        def _():
            remote(part.at[j], gathered.at[j], send1.at[j], recv1.at[j], device).wait_recv()

    peak = gathered[0]
    for j in range(1, 16):
        peak = jnp.maximum(peak, gathered[j])
    mass = jnp.zeros_like(peak)
    for j in range(16):
        mass = mass + jnp.exp2(gathered[j] - peak)
    transport = norm[...] - LN2 * (peak + jnp.log2(mass))
    new_pot = 0.5 * (pot[...] + transport)
    pot_out[...] = new_pot
    if not last:
        level[...] = LOG2E * (new_pot + weight[...] - norm[...])
        spread_start(pc, level, table, send2, recv2)
        spread_wait(pc, level, table, send2, recv2)
        level_out[...] = table[...]
    for j in range(16):
        device, mine = pc.owner(j)

        @pl.when(jnp.logical_not(mine))
        def _():
            remote(part.at[j], gathered.at[j], send1.at[j], recv1.at[j], device).wait_send()


def exchange(part, pot, weight, norm, step, last):
    DMA = pltpu.SemaphoreType.DMA
    vmem = pl.BlockSpec(memory_space=pltpu.VMEM)
    small = jax.ShapeDtypeStruct((16, 256), jnp.float32)
    big = jax.ShapeDtypeStruct((16, 16, 256), jnp.float32)
    if last:
        scratch = [pltpu.VMEM((16, 16, 256), jnp.float32), DMA((16,)), DMA((16,))]
        outs, specs = small, vmem
    else:
        scratch = [
            pltpu.VMEM((16, 16, 256), jnp.float32),
            pltpu.VMEM((16, 256), jnp.float32),
            pltpu.VMEM((16, 16, 256), jnp.float32),
            DMA((16,)),
            DMA((16,)),
            DMA((16,)),
            DMA((16,)),
        ]
        outs, specs = (small, big), (vmem, vmem)
    return pl.pallas_call(
        functools.partial(exchange_kernel, last),
        out_shape=outs,
        in_specs=[vmem] * 4,
        out_specs=specs,
        scratch_shapes=scratch,
        compiler_params=pltpu.CompilerParams(
            collective_id=1 + step, has_side_effects=True, vmem_limit_bytes=VMEM_CAP
        ),
        name="exchange_levels",
    )(part, pot, weight, norm)


def per_device(embeds, log_weights, listing):
    emb = embeds[0]
    pairs = listing[0]
    sq = jnp.sum(jnp.square(emb.astype(jnp.float32)), axis=2)
    norm = jnp.pad(INV_BLUR * sq, ((0, 4), (0, 0)))
    weight = jnp.pad(log_weights[0], ((0, 4), (0, 0)))
    own_local = pairs[:, 0] % 12
    far_dev = pairs[:, 1] // 12
    far_local = pairs[:, 1] % 12
    x0 = far_dev // 32
    y0 = (far_dev // 8) % 4
    z0 = far_dev % 8
    code = (z0 * 2 + (x0 + y0) % 2) * 2048 + own_local * 128 + (y0 * 2 + x0 // 2) * 16 + far_local
    code = jnp.pad(code.astype(jnp.float32), (0, 256 - code.shape[0]), constant_values=-1.0)
    level = LOG2E * (weight - norm)
    level = jnp.where(jnp.arange(16)[:, None] == 12, code[None, :], level)
    src, tgt, table, todo = gather(emb, level)
    pot = jnp.zeros_like(norm)
    for step in range(ITERS):
        part = pair_pass(todo, table, src, tgt)
        if step < ITERS - 1:
            pot, table = exchange(part, pot, weight, norm, step, False)
        else:
            pot = exchange(part, pot, weight, norm, step, True)
    return pot[None, :12]


def solution(mesh):
    placed = (
        P("side", ("group", "dev"), None, None),
        P("side", ("group", "dev"), None),
        P("side", ("group", "dev"), None),
    )
    return jax.shard_map(
        per_device,
        mesh=mesh,
        in_specs=placed,
        out_specs=P("side", ("group", "dev"), None),
        check_vma=False,
    )
```

```python
import functools
import math

import jax
import jax.numpy as jnp
from jax import lax
from jax.experimental import pallas as pl
from jax.experimental.pallas import tpu as pltpu
from jax.sharding import PartitionSpec as P

MESH = pl.DeviceIdType.MESH
ITERS = 3
WIDE = 4
DEPTH = 16
NX, NY, NZ = 4, 4, 8
LOG2E = math.log2(math.e)
LN2 = math.log(2.0)
INV_BLUR = 10.0
SCALE = 2.0 * INV_BLUR * LOG2E
EMPTY = -1e30
VMEM_CAP = 48 * 1024 * 1024


def where(pred, a, b):
    return jnp.where(pred, a, b)


class Place:
    def __init__(self):
        self.k = lax.axis_index("side")
        self.x = lax.axis_index("group")
        dev = lax.axis_index("dev")
        self.y = dev // NZ
        self.z = dev % NZ
        self.kq = (self.x + self.y) % 2
        self.own_slot = self.y * 2 + self.x // 2

    def dev(self, k, x, y, z):
        return (k, x, y * NZ + z)

    def owner(self, j):
        if j < 8:
            return self.dev(jnp.int32(0), self.x, self.y, jnp.int32(j)), jnp.logical_and(self.k == 0, self.z == j)
        d = j - 8
        y0 = d // 2
        x0 = 2 * (d % 2) + (y0 + self.k) % 2
        me = jnp.logical_and(self.k == 1, jnp.logical_and(self.x == x0, self.y == y0))
        return self.dev(jnp.int32(1), x0, jnp.int32(y0), self.z), me

    def meeter(self, j):
        src = self.k == 0
        kk = where(src, j % 2, self.kq)
        xx = where(src, self.x, j % 4)
        yy = where(src, self.y, j // 4)
        zz = where(src, j // 2, self.z)
        me = jnp.logical_and(
            jnp.logical_and(kk == self.k, xx == self.x), jnp.logical_and(yy == self.y, zz == self.z)
        )
        return self.dev(kk, xx, yy, zz), me

    def peers(self):
        return 16 - where(jnp.logical_or(self.k == 0, self.kq == 1), 1, 0)

    def level_slot(self):
        return where(self.k == 0, self.z, 8 + self.own_slot)

    def meet_slot(self, j):
        return self.z * 2 + self.k if j < 8 else self.y * 4 + self.x


def remote(src, dst, send_sem, recv_sem, device):
    return pltpu.make_async_remote_copy(
        src_ref=src, dst_ref=dst, send_sem=send_sem, recv_sem=recv_sem, device_id=device, device_id_type=MESH
    )


def spread_start(pc, level, table, send_sem, recv_sem):
    slot = pc.level_slot()
    for j in range(16):
        device, me = pc.meeter(j)

        @pl.when(jnp.logical_not(me))
        def _():
            remote(level, table.at[slot], send_sem.at[j], recv_sem.at[slot], device).start()

        @pl.when(me)
        def _():
            table[slot] = level[...]


def spread_wait(pc, level, table, send_sem, recv_sem):
    for j in range(16):
        device, me = pc.meeter(j)
        owner, mine = pc.owner(j)

        @pl.when(jnp.logical_not(mine))
        def _():
            remote(level, table.at[j], send_sem.at[j], recv_sem.at[j], owner).wait_recv()

    for j in range(16):
        device, me = pc.meeter(j)

        @pl.when(jnp.logical_not(me))
        def _():
            remote(level, table.at[j], send_sem.at[j], recv_sem.at[j], device).wait_send()


def signal(sem, device):
    pl.semaphore_signal(sem, inc=1, device_id=device, device_id_type=MESH)


def gather_kernel(
    emb, level, src_out, tgt_out, level_out, list_out,
    table, local_sem, own_sem, z_send, z_recv, sib_send, sib_recv,
    first_send, first_recv, next_send, next_recv, relay_send, relay_recv, lv_send, lv_recv,
):
    pc = Place()
    k, x, y, z = pc.k, pc.x, pc.y, pc.z
    sibling = pc.dev(1 - k, x, y, z)
    zdev = [pc.dev(k, x, y, (z + 1) % NZ), pc.dev(k, x, y, (z + NZ - 1) % NZ)]
    xdev = [pc.dev(k, (x + 1) % NX, y, z), pc.dev(k, (x + NX - 1) % NX, y, z)]
    ydev = [pc.dev(k, x, (y + 1) % NY, z), pc.dev(k, x, (y + NY - 1) % NY, z)]

    barrier = pltpu.get_barrier_semaphore()
    for device in [sibling] + zdev + xdev + ydev:
        signal(barrier, device)
    for j in range(16):
        device, mine = pc.owner(j)

        @pl.when(jnp.logical_not(mine))
        def _():
            signal(barrier, device)

    pl.semaphore_wait(barrier, 7 + pc.peers())

    native = k == pc.kq

    def src_at(h, z0, s):
        return src_out.at[h, z0, pl.ds(3 * s, 3)]

    def tgt_at(f, line, o, s):
        return tgt_out.at[f, line, o, pl.ds(3 * s, 3)]

    line_of = [y, x]
    spot_of = [x, y]
    spread_dev = [xdev, ydev]
    onward_dev = [ydev, xdev]

    @pl.when(k == 0)
    def _():
        for h in (1, 0):
            for s in range(2):
                part = emb.at[pl.ds(6 * h + 3 * s, 3)]
                remote(part, src_at(h, z, s), own_sem.at[0, h, s], own_sem.at[1, h, s], sibling).start()
        for h in range(2):
            for s in range(2):
                part = emb.at[pl.ds(6 * h + 3 * s, 3)]
                pltpu.make_async_copy(part, src_at(h, z, s), local_sem.at[h, s]).start()

    @pl.when(jnp.logical_and(k == 1, pc.kq == 1))
    def _():
        for f in range(2):
            for s in range(2):
                part = emb.at[pl.ds(6 * f + 3 * s, 3)]
                pltpu.make_async_copy(part, tgt_at(f, line_of[f], spot_of[f] // 2, s), local_sem.at[f, s]).start()

    @pl.when(jnp.logical_and(k == 1, pc.kq == 0))
    def _():
        for f in range(2):
            for s in range(2):
                part = emb.at[pl.ds(6 * f + 3 * s, 3)]
                remote(
                    part, tgt_at(f, line_of[f], spot_of[f] // 2, s), own_sem.at[0, f, s], own_sem.at[1, f, s], sibling
                ).start()

    spread_start(pc, level, table, lv_send, lv_recv)

    def z_copy(way, r, s):
        z0 = (z - r + NZ) % NZ if way == 0 else (z + r) % NZ
        part = src_out.at[k, z0, pl.ds(3 * s, 3)]
        return remote(part, part, z_send.at[way, r, s], z_recv.at[way, r, s], zdev[way])

    def z_landed(way, r, s):
        z0 = (z - r - 1 + NZ) % NZ if way == 0 else (z + r + 1) % NZ
        part = src_out.at[k, z0, pl.ds(3 * s, 3)]
        return remote(part, part, z_send.at[way, r, s], z_recv.at[way, r, s], zdev[way])

    def sib_copy(way, r, s):
        z0 = (z - r - 1 + NZ) % NZ if way == 0 else (z + r + 1) % NZ
        part = src_out.at[k, z0, pl.ds(3 * s, 3)]
        return remote(part, part, sib_send.at[way, r, s], sib_recv.at[way, r, s], sibling)

    def sib_landed(way, r, s):
        z0 = (z - r - 1 + NZ) % NZ if way == 0 else (z + r + 1) % NZ
        part = src_out.at[1 - k, z0, pl.ds(3 * s, 3)]
        return remote(part, part, sib_send.at[way, r, s], sib_recv.at[way, r, s], sibling)

    def z_subs(way, r):
        return (0, 1) if r < 3 else (way,)

    for s in range(2):
        @pl.when(k == 0)
        def _():
            part = emb.at[pl.ds(3 * s, 3)]
            pltpu.make_async_copy(part, src_at(0, z, s), local_sem.at[0, s]).wait()

        @pl.when(k == 1)
        def _():
            part = src_at(1, z, s)
            remote(part, part, own_sem.at[0, 1, s], own_sem.at[1, 1, s], sibling).wait_recv()

        for way in range(2):
            z_copy(way, 0, s).start()

    def first_copy(f, way, o, s):
        part = tgt_at(f, line_of[f], o, s)
        return remote(part, part, first_send.at[f, way, s], first_recv.at[f, way, s], spread_dev[f][way])

    def next_copy(f, way, o, s):
        part = tgt_at(f, line_of[f], o, s)
        return remote(part, part, next_send.at[f, way, o, s], next_recv.at[f, way, o, s], onward_dev[f][way])

    def from_line(f, way):
        n = line_of[f]
        return (n + 3) % 4 if way == 0 else (n + 1) % 4

    def next_landed(f, way, o, s):
        part = tgt_at(f, from_line(f, way), o, s)
        return remote(part, part, next_send.at[f, way, o, s], next_recv.at[f, way, o, s], onward_dev[f][way])

    def relay_copy(f, way, o):
        part = tgt_at(f, from_line(f, way), o, way)
        return remote(part, part, relay_send.at[f, way, o], relay_recv.at[f, way, o], onward_dev[f][way])

    def relay_landed(f, way, o):
        part = tgt_at(f, (line_of[f] + 2) % 4, o, way)
        return remote(part, part, relay_send.at[f, way, o], relay_recv.at[f, way, o], onward_dev[f][way])

    home = [spot_of[f] // 2 for f in range(2)]
    near = [[((spot_of[f] + 3) % 4) // 2, ((spot_of[f] + 1) % 4) // 2] for f in range(2)]

    @pl.when(native)
    def _():
        for s in range(2):
            for f in range(2):
                part = tgt_at(f, line_of[f], home[f], s)

                @pl.when(k == 1)
                def _():
                    pltpu.make_async_copy(emb.at[pl.ds(6 * f + 3 * s, 3)], part, local_sem.at[f, s]).wait()

                @pl.when(k == 0)
                def _():
                    remote(part, part, own_sem.at[0, f, s], own_sem.at[1, f, s], sibling).wait_recv()

                for way in range(2):
                    first_copy(f, way, home[f], s).start()
        for s in range(2):
            for f in range(2):
                for way in range(2):
                    next_copy(f, way, home[f], s).start()

    def z_forward(r):
        for s in range(2):
            for way in range(2):
                if s in z_subs(way, r):
                    z_landed(way, r, s).wait_recv()
                    if r < 3 and s in z_subs(way, r + 1):
                        z_copy(way, r + 1, s).start()
                    sib_copy(way, r, s).start()

    z_forward(0)

    @pl.when(jnp.logical_not(native))
    def _():
        for s in range(2):
            for f in range(2):
                for way in range(2):
                    o = near[f][way]
                    first_copy(f, way, o, s).wait_recv()
                    if s == way:
                        first_copy(f, way, o, s).start()
                    for w in range(2):
                        next_copy(f, w, o, s).start()

    z_forward(1)

    @pl.when(native)
    def _():
        for f in range(2):
            for way in range(2):
                o = 1 - home[f]
                first_copy(f, way, o, way).wait_recv()
                for w in range(2):
                    next_copy(f, w, o, way).start()

    def onward(nth):
        for s in range(2):
            for f in range(2):
                o = home[f] if nth == 0 else 1 - home[f]
                for way in range(2):
                    next_landed(f, way, o, s).wait_recv()
                    if s == way:
                        relay_copy(f, way, o).start()

    onward(0)
    z_forward(2)
    onward(1)
    z_forward(3)

    spread_wait(pc, level, table, lv_send, lv_recv)
    level_out[...] = table[...]
    codes = table[0:8, 12, 0:128]
    low = ((z * 2 + k) * 2048).astype(jnp.float32)
    mine = jnp.logical_and(codes >= low, codes < low + 2048.0)
    hit = jnp.where(mine, 1.0, 0.0)
    row_id = lax.broadcasted_iota(jnp.int32, (128, 128), 0)
    col_id = lax.broadcasted_iota(jnp.int32, (128, 128), 1)
    upper = jnp.where(row_id < col_id, 1.0, 0.0)
    within = jnp.dot(hit, upper, preferred_element_type=jnp.float32)
    totals = jnp.broadcast_to(jnp.sum(hit, axis=1, keepdims=True), (8, 128))
    below = jnp.where(
        lax.broadcasted_iota(jnp.int32, (8, 8), 1) < lax.broadcasted_iota(jnp.int32, (8, 8), 0), 1.0, 0.0
    )
    before = jnp.dot(below, totals, preferred_element_type=jnp.float32, precision=lax.Precision.HIGHEST)
    rank = jnp.where(mine, within + before, -1.0)
    packed = codes - low + 2048.0 * lax.broadcasted_iota(jnp.int32, (8, 128), 0).astype(jnp.float32)
    want = row_id.astype(jnp.float32)
    picked = jnp.zeros((128, 128), jnp.float32)
    for r in range(8):
        picked = picked + jnp.where(want == rank[r : r + 1, :], packed[r : r + 1, :], 0.0)
    entries = jnp.broadcast_to(jnp.sum(picked, axis=1, keepdims=True), (128, 128))
    line = jnp.sum(jnp.where(row_id == col_id, entries, 0.0), axis=0, keepdims=True)
    count = jnp.broadcast_to(jnp.sum(totals[:, 0:1], axis=0, keepdims=True), (1, 128))
    list_out[...] = jnp.concatenate([line, count, jnp.zeros((6, 128), jnp.float32)], axis=0).astype(jnp.int32)

    for f in range(2):
        for way in range(2):
            for o in range(2):
                relay_landed(f, way, o).wait_recv()
    for r in range(4):
        for way in range(2):
            for s in z_subs(way, r):
                sib_landed(way, r, s).wait_recv()

    @pl.when(k == 1)
    def _():
        for s in range(2):
            part = src_at(0, z, s)
            remote(part, part, own_sem.at[0, 0, s], own_sem.at[1, 0, s], sibling).wait_recv()

    @pl.when(k == 0)
    def _():
        for s in range(2):
            part = emb.at[pl.ds(6 + 3 * s, 3)]
            pltpu.make_async_copy(part, src_at(1, z, s), local_sem.at[1, s]).wait()
        for h in range(2):
            for s in range(2):
                part = emb.at[pl.ds(6 * h + 3 * s, 3)]
                remote(part, src_at(h, z, s), own_sem.at[0, h, s], own_sem.at[1, h, s], sibling).wait_send()

    @pl.when(jnp.logical_and(k == 1, pc.kq == 0))
    def _():
        for f in range(2):
            for s in range(2):
                part = emb.at[pl.ds(6 * f + 3 * s, 3)]
                remote(
                    part, tgt_at(f, line_of[f], home[f], s), own_sem.at[0, f, s], own_sem.at[1, f, s], sibling
                ).wait_send()

    for r in range(4):
        for way in range(2):
            for s in z_subs(way, r):
                z_copy(way, r, s).wait_send()
                sib_copy(way, r, s).wait_send()
    for f in range(2):
        for way in range(2):
            for s in range(2):
                @pl.when(native)
                def _():
                    first_copy(f, way, home[f], s).wait_send()

            @pl.when(jnp.logical_not(native))
            def _():
                first_copy(f, way, near[f][way], way).wait_send()

            for o in range(2):
                relay_copy(f, way, o).wait_send()
                for s in range(2):
                    next_copy(f, way, o, s).wait_send()


def gather(emb, level):
    DMA = pltpu.SemaphoreType.DMA
    any_spec = pl.BlockSpec(memory_space=pl.ANY)
    vmem = pl.BlockSpec(memory_space=pltpu.VMEM)
    return pl.pallas_call(
        gather_kernel,
        out_shape=(
            jax.ShapeDtypeStruct((2, 8, 6, 256, 256), jnp.bfloat16),
            jax.ShapeDtypeStruct((2, 4, 2, 6, 256, 256), jnp.bfloat16),
            jax.ShapeDtypeStruct((16, 16, 256), jnp.float32),
            jax.ShapeDtypeStruct((8, 128), jnp.int32),
        ),
        in_specs=[any_spec, vmem],
        out_specs=(any_spec, any_spec, vmem, vmem),
        scratch_shapes=[
            pltpu.VMEM((16, 16, 256), jnp.float32),
            DMA((2, 2)),
            DMA((2, 2, 2)),
            DMA((2, 4, 2)),
            DMA((2, 4, 2)),
            DMA((2, 4, 2)),
            DMA((2, 4, 2)),
            DMA((2, 2, 2)),
            DMA((2, 2, 2)),
            DMA((2, 2, 2, 2)),
            DMA((2, 2, 2, 2)),
            DMA((2, 2, 2)),
            DMA((2, 2, 2)),
            DMA((16,)),
            DMA((16,)),
        ],
        compiler_params=pltpu.CompilerParams(collective_id=0, has_side_effects=True, vmem_limit_bytes=VMEM_CAP),
        name="gather_blocks",
    )(emb, level)


def pair_kernel(pairs, level, src, tgt, part_out, xbuf, ybuf, turned, top, total, sems):
    k = lax.axis_index("side")

    def fetch(p, slot):
        code = pairs[0, p]
        bs = code // 128
        bt = code % 128
        sz = bs // 16
        sb = bs % 16
        d = bt // 16
        tb = bt % 16
        y0 = d // 2
        x0 = 2 * (d % 2) + (y0 + k) % 2
        f = tb // 6
        line = where(f == 0, y0, x0)
        o = where(f == 0, x0, y0) // 2
        return (
            pltpu.make_async_copy(src.at[sb // 6, sz, sb % 6], xbuf.at[slot], sems.at[0, slot]),
            pltpu.make_async_copy(tgt.at[f, line, o, tb % 6], ybuf.at[slot], sems.at[1, slot]),
        )

    count = pairs[1, 0]
    rounds = (count + WIDE - 1) // WIDE

    def fetch_round(r):
        for u in range(WIDE):
            p = r * WIDE + u
            for copy in fetch(p, p % DEPTH):
                copy.start()

    for r in range(DEPTH // WIDE - 1):
        @pl.when(r < rounds)
        def _():
            fetch_round(r)

    for g in range(2):
        rows = level[8 * g : 8 * g + 8].reshape(128, 256)
        turned[g] = rows.T
    top[...] = jnp.full(top.shape, EMPTY, jnp.float32)
    total[...] = jnp.zeros(total.shape, jnp.float32)
    lane = lax.broadcasted_iota(jnp.int32, (256, 128), 1)
    contract = (((1,), (1,)), ((), ()))

    def sums(a, b, g_from, index_from):
        bias = jnp.sum(jnp.where(lane == index_from, turned[g_from], 0.0), axis=1, keepdims=True)
        score = lax.dot_general(a, b, contract, preferred_element_type=jnp.float32) * SCALE + bias
        peak = jnp.max(score, axis=0, keepdims=True)
        return peak, jnp.sum(jnp.exp2(score - peak), axis=0, keepdims=True)

    def merge(peak, mass, g_to, index_to):
        old_peak = top[g_to, pl.ds(index_to, 1), :]
        old_mass = total[g_to, pl.ds(index_to, 1), :]
        new_peak = jnp.maximum(old_peak, peak)
        top[g_to, pl.ds(index_to, 1), :] = new_peak
        total[g_to, pl.ds(index_to, 1), :] = old_mass * jnp.exp2(old_peak - new_peak) + mass * jnp.exp2(peak - new_peak)

    def body(r, carry):
        @pl.when(r + DEPTH // WIDE - 1 < rounds)
        def _():
            fetch_round(r + DEPTH // WIDE - 1)

        for u in range(WIDE):
            p = r * WIDE + u
            for copy in fetch(p, p % DEPTH):
                copy.wait()
        found = []
        for u in range(WIDE):
            p = r * WIDE + u
            code = pairs[0, p]
            xs = xbuf[p % DEPTH]
            ys = ybuf[p % DEPTH]
            found.append((p, code, sums(xs, ys, 0, code // 128), sums(ys, xs, 1, code % 128)))
        for p, code, down, across in found:
            live = p < count
            for (peak, mass), g_to, index_to in ((down, 1, code % 128), (across, 0, code // 128)):
                merge(where(live, peak, EMPTY), where(live, mass, 0.0), g_to, index_to)
        return carry

    lax.fori_loop(0, rounds, body, 0)
    for g in range(2):
        mass = total[g]
        value = jnp.where(mass > 0.0, top[g] + jnp.log2(jnp.maximum(mass, 1e-37)), EMPTY)
        part_out[8 * g : 8 * g + 8] = value.reshape(8, 16, 256)


def pair_pass(pairs, level, src, tgt):
    any_spec = pl.BlockSpec(memory_space=pl.ANY)
    vmem = pl.BlockSpec(memory_space=pltpu.VMEM)
    return pl.pallas_call(
        pair_kernel,
        out_shape=jax.ShapeDtypeStruct((16, 16, 256), jnp.float32),
        in_specs=[pl.BlockSpec(memory_space=pltpu.SMEM), vmem, any_spec, any_spec],
        out_specs=vmem,
        scratch_shapes=[
            pltpu.VMEM((DEPTH, 256, 256), jnp.bfloat16),
            pltpu.VMEM((DEPTH, 256, 256), jnp.bfloat16),
            pltpu.VMEM((2, 256, 128), jnp.float32),
            pltpu.VMEM((2, 128, 256), jnp.float32),
            pltpu.VMEM((2, 128, 256), jnp.float32),
            pltpu.SemaphoreType.DMA((2, DEPTH)),
        ],
        compiler_params=pltpu.CompilerParams(vmem_limit_bytes=VMEM_CAP),
        name="pair_sums",
    )(pairs, level, src, tgt)


def exchange_kernel(last, part, pot, weight, norm, *rest):
    if last:
        pot_out, gathered, send1, recv1 = rest
    else:
        pot_out, level_out, gathered, level, table, send1, recv1, send2, recv2 = rest
    pc = Place()
    barrier = pltpu.get_barrier_semaphore()
    for j in range(16):
        device, me = pc.meeter(j)

        @pl.when(jnp.logical_not(me))
        def _():
            signal(barrier, device)

    pl.semaphore_wait(barrier, pc.peers())

    for j in range(16):
        device, mine = pc.owner(j)
        slot = pc.meet_slot(j)

        @pl.when(jnp.logical_not(mine))
        def _():
            remote(part.at[j], gathered.at[slot], send1.at[j], recv1.at[slot], device).start()

        @pl.when(mine)
        def _():
            gathered[slot] = part[j]

    for j in range(16):
        device, me = pc.meeter(j)

        @pl.when(jnp.logical_not(me))
        def _():
            remote(part.at[j], gathered.at[j], send1.at[j], recv1.at[j], device).wait_recv()

    peak = gathered[0]
    for j in range(1, 16):
        peak = jnp.maximum(peak, gathered[j])
    mass = jnp.zeros_like(peak)
    for j in range(16):
        mass = mass + jnp.exp2(gathered[j] - peak)
    transport = norm[...] - LN2 * (peak + jnp.log2(mass))
    new_pot = 0.5 * (pot[...] + transport)
    pot_out[...] = new_pot
    if not last:
        level[...] = LOG2E * (new_pot + weight[...] - norm[...])
        spread_start(pc, level, table, send2, recv2)
        spread_wait(pc, level, table, send2, recv2)
        level_out[...] = table[...]
    for j in range(16):
        device, mine = pc.owner(j)

        @pl.when(jnp.logical_not(mine))
        def _():
            remote(part.at[j], gathered.at[j], send1.at[j], recv1.at[j], device).wait_send()


def exchange(part, pot, weight, norm, step, last):
    DMA = pltpu.SemaphoreType.DMA
    vmem = pl.BlockSpec(memory_space=pltpu.VMEM)
    small = jax.ShapeDtypeStruct((16, 256), jnp.float32)
    big = jax.ShapeDtypeStruct((16, 16, 256), jnp.float32)
    if last:
        scratch = [pltpu.VMEM((16, 16, 256), jnp.float32), DMA((16,)), DMA((16,))]
        outs, specs = small, vmem
    else:
        scratch = [
            pltpu.VMEM((16, 16, 256), jnp.float32),
            pltpu.VMEM((16, 256), jnp.float32),
            pltpu.VMEM((16, 16, 256), jnp.float32),
            DMA((16,)),
            DMA((16,)),
            DMA((16,)),
            DMA((16,)),
        ]
        outs, specs = (small, big), (vmem, vmem)
    return pl.pallas_call(
        functools.partial(exchange_kernel, last),
        out_shape=outs,
        in_specs=[vmem] * 4,
        out_specs=specs,
        scratch_shapes=scratch,
        compiler_params=pltpu.CompilerParams(
            collective_id=1 + step, has_side_effects=True, vmem_limit_bytes=VMEM_CAP
        ),
        name="exchange_levels",
    )(part, pot, weight, norm)


def per_device(embeds, log_weights, listing):
    emb = embeds[0]
    pairs = listing[0]
    sq = jnp.sum(jnp.square(emb.astype(jnp.float32)), axis=2)
    norm = jnp.pad(INV_BLUR * sq, ((0, 4), (0, 0)))
    weight = jnp.pad(log_weights[0], ((0, 4), (0, 0)))
    own_local = pairs[:, 0] % 12
    far_dev = pairs[:, 1] // 12
    far_local = pairs[:, 1] % 12
    x0 = far_dev // 32
    y0 = (far_dev // 8) % 4
    z0 = far_dev % 8
    code = (z0 * 2 + (x0 + y0) % 2) * 2048 + own_local * 128 + (y0 * 2 + x0 // 2) * 16 + far_local
    code = jnp.pad(code.astype(jnp.float32), (0, 256 - code.shape[0]), constant_values=-1.0)
    level = LOG2E * (weight - norm)
    level = jnp.where(jnp.arange(16)[:, None] == 12, code[None, :], level)
    src, tgt, table, todo = gather(emb, level)
    pot = jnp.zeros_like(norm)
    for step in range(ITERS):
        part = pair_pass(todo, table, src, tgt)
        if step < ITERS - 1:
            pot, table = exchange(part, pot, weight, norm, step, False)
        else:
            pot = exchange(part, pot, weight, norm, step, True)
    return pot[None, :12]


def solution(mesh):
    placed = (
        P("side", ("group", "dev"), None, None),
        P("side", ("group", "dev"), None),
        P("side", ("group", "dev"), None),
    )
    return jax.shard_map(
        per_device,
        mesh=mesh,
        in_specs=placed,
        out_specs=P("side", ("group", "dev"), None),
        check_vma=False,
    )
```

```python
import math

import jax
import jax.numpy as jnp
from jax import lax
from jax.experimental import pallas as pl
from jax.experimental.pallas import tpu as pltpu
from jax.sharding import PartitionSpec as P

MESH = pl.DeviceIdType.MESH
ITERS = 3
NX, NY, NZ = 4, 4, 8
LOG2E = math.log2(math.e)
LN2 = math.log(2.0)
INV_BLUR = 10.0
SCALE = 2.0 * INV_BLUR * LOG2E
EMPTY = -1e30
VMEM_CAP = 50 * 1024 * 1024


def where(pred, a, b):
    return jnp.where(pred, a, b)


class Place:
    def __init__(self):
        self.k = lax.axis_index("side")
        self.x = lax.axis_index("group")
        dev = lax.axis_index("dev")
        self.y = dev // NZ
        self.z = dev % NZ
        self.kq = (self.x + self.y) % 2
        self.own_slot = self.y * 2 + self.x // 2

    def dev(self, k, x, y, z):
        return (k, x, y * NZ + z)

    def owner(self, j):
        if j < 8:
            return self.dev(jnp.int32(0), self.x, self.y, jnp.int32(j)), jnp.logical_and(self.k == 0, self.z == j)
        d = j - 8
        y0 = d // 2
        x0 = 2 * (d % 2) + (y0 + self.k) % 2
        me = jnp.logical_and(self.k == 1, jnp.logical_and(self.x == x0, self.y == y0))
        return self.dev(jnp.int32(1), x0, jnp.int32(y0), self.z), me

    def meeter(self, j):
        src = self.k == 0
        kk = where(src, j % 2, self.kq)
        xx = where(src, self.x, j % 4)
        yy = where(src, self.y, j // 4)
        zz = where(src, j // 2, self.z)
        me = jnp.logical_and(
            jnp.logical_and(kk == self.k, xx == self.x), jnp.logical_and(yy == self.y, zz == self.z)
        )
        return self.dev(kk, xx, yy, zz), me

    def peers(self):
        return 16 - where(jnp.logical_or(self.k == 0, self.kq == 1), 1, 0)

    def level_slot(self):
        return where(self.k == 0, self.z, 8 + self.own_slot)

    def meet_slot(self, j):
        return self.z * 2 + self.k if j < 8 else self.y * 4 + self.x


def remote(src, dst, send_sem, recv_sem, device):
    return pltpu.make_async_remote_copy(
        src_ref=src, dst_ref=dst, send_sem=send_sem, recv_sem=recv_sem, device_id=device, device_id_type=MESH
    )


def spread_start(pc, level, table, send_sem, recv_sem):
    slot = pc.level_slot()
    for j in range(16):
        device, me = pc.meeter(j)

        @pl.when(jnp.logical_not(me))
        def _():
            remote(level, table.at[slot], send_sem.at[j], recv_sem.at[slot], device).start()

        @pl.when(me)
        def _():
            table[slot] = level[...]


def spread_wait(pc, level, table, send_sem, recv_sem):
    for j in range(16):
        device, me = pc.meeter(j)
        owner, mine = pc.owner(j)

        @pl.when(jnp.logical_not(mine))
        def _():
            remote(level, table.at[j], send_sem.at[j], recv_sem.at[j], owner).wait_recv()

    for j in range(16):
        device, me = pc.meeter(j)

        @pl.when(jnp.logical_not(me))
        def _():
            remote(level, table.at[j], send_sem.at[j], recv_sem.at[j], device).wait_send()


def signal(sem, device):
    pl.semaphore_signal(sem, inc=1, device_id=device, device_id_type=MESH)


def sinkhorn_kernel(
    emb, meet, weight, norm, pot_out,
    src, tgt, table, level, plan, todo, turned, parts, gathered, pot, found,
    todo_sem, local_sem, own_sem, z_send, z_recv, sib_send, sib_recv,
    first_send, first_recv, next_send, next_recv, relay_send, relay_recv,
    plan_send, plan_recv, lv_send, lv_recv, part_send, part_recv,
):
    pc = Place()
    k, x, y, z = pc.k, pc.x, pc.y, pc.z
    sibling = pc.dev(1 - k, x, y, z)
    zdev = [pc.dev(k, x, y, (z + 1) % NZ), pc.dev(k, x, y, (z + NZ - 1) % NZ)]
    xdev = [pc.dev(k, (x + 1) % NX, y, z), pc.dev(k, (x + NX - 1) % NX, y, z)]
    ydev = [pc.dev(k, x, (y + 1) % NY, z), pc.dev(k, x, (y + NY - 1) % NY, z)]

    barrier = pltpu.get_barrier_semaphore()
    for device in [sibling] + zdev + xdev + ydev:
        signal(barrier, device)
    for j in range(16):
        device, mine = pc.owner(j)

        @pl.when(jnp.logical_not(mine))
        def _():
            signal(barrier, device)

    pl.semaphore_wait(barrier, 7 + pc.peers())

    native = k == pc.kq

    def src_at(h, z0, s):
        return src.at[z0, pl.ds(6 * h + 3 * s, 3)]

    def tgt_at(f, line, o, s, core=k):
        if f == 0:
            return tgt.at[line * 2 + o, pl.ds(3 * s, 3)]
        return tgt.at[(2 * o + (line + core) % 2) * 2 + line // 2, pl.ds(6 + 3 * s, 3)]

    line_of = [y, x]
    spot_of = [x, y]
    spread_dev = [xdev, ydev]
    onward_dev = [ydev, xdev]

    @pl.when(k == 0)
    def _():
        for h in (1, 0):
            for s in range(2):
                part = emb.at[pl.ds(6 * h + 3 * s, 3)]
                remote(part, src_at(h, z, s), own_sem.at[0, h, s], own_sem.at[1, h, s], sibling).start()
        for h in range(2):
            for s in range(2):
                part = emb.at[pl.ds(6 * h + 3 * s, 3)]
                pltpu.make_async_copy(part, src_at(h, z, s), local_sem.at[h, s]).start()

    @pl.when(jnp.logical_and(k == 1, pc.kq == 1))
    def _():
        for f in range(2):
            for s in range(2):
                part = emb.at[pl.ds(6 * f + 3 * s, 3)]
                pltpu.make_async_copy(part, tgt_at(f, line_of[f], spot_of[f] // 2, s), local_sem.at[f, s]).start()

    @pl.when(jnp.logical_and(k == 1, pc.kq == 0))
    def _():
        for f in range(2):
            for s in range(2):
                part = emb.at[pl.ds(6 * f + 3 * s, 3)]
                remote(
                    part, tgt_at(f, line_of[f], spot_of[f] // 2, s, pc.kq), own_sem.at[0, f, s], own_sem.at[1, f, s], sibling
                ).start()

    level[...] = LOG2E * (weight[...] - norm[...])
    spread_start(pc, level, table.at[0], lv_send.at[0], lv_recv.at[0])

    def plan_copy(j, slot, device):
        return remote(meet.at[j], plan.at[slot], plan_send.at[j], plan_recv.at[slot], device)

    @pl.when(k == 0)
    def _():
        for j in range(16):
            device, me = pc.meeter(j)

            @pl.when(jnp.logical_not(me))
            def _():
                plan_copy(j, z, device).start()

            @pl.when(me)
            def _():
                plan[z] = meet[j]

    def z_copy(way, r, s):
        z0 = (z - r + NZ) % NZ if way == 0 else (z + r) % NZ
        part = src.at[z0, pl.ds(6 * k + 3 * s, 3)]
        return remote(part, part, z_send.at[way, r, s], z_recv.at[way, r, s], zdev[way])

    def z_landed(way, r, s):
        z0 = (z - r - 1 + NZ) % NZ if way == 0 else (z + r + 1) % NZ
        part = src.at[z0, pl.ds(6 * k + 3 * s, 3)]
        return remote(part, part, z_send.at[way, r, s], z_recv.at[way, r, s], zdev[way])

    def sib_copy(way, r, s):
        z0 = (z - r - 1 + NZ) % NZ if way == 0 else (z + r + 1) % NZ
        part = src.at[z0, pl.ds(6 * k + 3 * s, 3)]
        return remote(part, part, sib_send.at[way, r, s], sib_recv.at[way, r, s], sibling)

    def sib_landed(way, r, s):
        z0 = (z - r - 1 + NZ) % NZ if way == 0 else (z + r + 1) % NZ
        part = src.at[z0, pl.ds(6 * (1 - k) + 3 * s, 3)]
        return remote(part, part, sib_send.at[way, r, s], sib_recv.at[way, r, s], sibling)

    def z_subs(way, r):
        return (0, 1) if r < 3 else (way,)

    for s in range(2):
        @pl.when(k == 0)
        def _():
            part = emb.at[pl.ds(3 * s, 3)]
            pltpu.make_async_copy(part, src_at(0, z, s), local_sem.at[0, s]).wait()

        @pl.when(k == 1)
        def _():
            part = src_at(1, z, s)
            remote(part, part, own_sem.at[0, 1, s], own_sem.at[1, 1, s], sibling).wait_recv()

        for way in range(2):
            z_copy(way, 0, s).start()

    def first_copy(f, way, o, s):
        part = tgt_at(f, line_of[f], o, s)
        return remote(part, part, first_send.at[f, way, s], first_recv.at[f, way, s], spread_dev[f][way])

    def next_copy(f, way, o, s):
        part = tgt_at(f, line_of[f], o, s)
        return remote(part, part, next_send.at[f, way, o, s], next_recv.at[f, way, o, s], onward_dev[f][way])

    def from_line(f, way):
        n = line_of[f]
        return (n + 3) % 4 if way == 0 else (n + 1) % 4

    def next_landed(f, way, o, s):
        part = tgt_at(f, from_line(f, way), o, s)
        return remote(part, part, next_send.at[f, way, o, s], next_recv.at[f, way, o, s], onward_dev[f][way])

    def relay_copy(f, way, o):
        part = tgt_at(f, from_line(f, way), o, way)
        return remote(part, part, relay_send.at[f, way, o], relay_recv.at[f, way, o], onward_dev[f][way])

    def relay_landed(f, way, o):
        part = tgt_at(f, (line_of[f] + 2) % 4, o, way)
        return remote(part, part, relay_send.at[f, way, o], relay_recv.at[f, way, o], onward_dev[f][way])

    home = [spot_of[f] // 2 for f in range(2)]
    near = [[((spot_of[f] + 3) % 4) // 2, ((spot_of[f] + 1) % 4) // 2] for f in range(2)]

    @pl.when(native)
    def _():
        for s in range(2):
            for f in range(2):
                part = tgt_at(f, line_of[f], home[f], s)

                @pl.when(k == 1)
                def _():
                    pltpu.make_async_copy(emb.at[pl.ds(6 * f + 3 * s, 3)], part, local_sem.at[f, s]).wait()

                @pl.when(k == 0)
                def _():
                    remote(part, part, own_sem.at[0, f, s], own_sem.at[1, f, s], sibling).wait_recv()

                for way in range(2):
                    first_copy(f, way, home[f], s).start()
        for s in range(2):
            for f in range(2):
                for way in range(2):
                    next_copy(f, way, home[f], s).start()

    def z_forward(r):
        for s in range(2):
            for way in range(2):
                if s in z_subs(way, r):
                    z_landed(way, r, s).wait_recv()
                    if r < 3 and s in z_subs(way, r + 1):
                        z_copy(way, r + 1, s).start()
                    sib_copy(way, r, s).start()

    z_forward(0)

    @pl.when(jnp.logical_not(native))
    def _():
        for s in range(2):
            for f in range(2):
                for way in range(2):
                    o = near[f][way]
                    first_copy(f, way, o, s).wait_recv()
                    if s == way:
                        first_copy(f, way, o, s).start()
                    for w in range(2):
                        next_copy(f, w, o, s).start()

    z_forward(1)

    @pl.when(native)
    def _():
        for f in range(2):
            for way in range(2):
                o = 1 - home[f]
                first_copy(f, way, o, way).wait_recv()
                for w in range(2):
                    next_copy(f, w, o, way).start()

    def onward(nth):
        for s in range(2):
            for f in range(2):
                o = home[f] if nth == 0 else 1 - home[f]
                for way in range(2):
                    next_landed(f, way, o, s).wait_recv()
                    if s == way:
                        relay_copy(f, way, o).start()

    onward(0)
    z_forward(2)
    onward(1)
    z_forward(3)

    for f in range(2):
        for way in range(2):
            for o in range(2):
                relay_landed(f, way, o).wait_recv()
    for r in range(4):
        for way in range(2):
            for s in z_subs(way, r):
                sib_landed(way, r, s).wait_recv()

    @pl.when(k == 1)
    def _():
        for s in range(2):
            part = src_at(0, z, s)
            remote(part, part, own_sem.at[0, 0, s], own_sem.at[1, 0, s], sibling).wait_recv()

    @pl.when(k == 0)
    def _():
        for s in range(2):
            part = emb.at[pl.ds(6 + 3 * s, 3)]
            pltpu.make_async_copy(part, src_at(1, z, s), local_sem.at[1, s]).wait()
        for h in range(2):
            for s in range(2):
                part = emb.at[pl.ds(6 * h + 3 * s, 3)]
                remote(part, src_at(h, z, s), own_sem.at[0, h, s], own_sem.at[1, h, s], sibling).wait_send()

    @pl.when(jnp.logical_and(k == 1, pc.kq == 0))
    def _():
        for f in range(2):
            for s in range(2):
                part = emb.at[pl.ds(6 * f + 3 * s, 3)]
                remote(
                    part, tgt_at(f, line_of[f], home[f], s, pc.kq), own_sem.at[0, f, s], own_sem.at[1, f, s], sibling
                ).wait_send()

    for r in range(4):
        for way in range(2):
            for s in z_subs(way, r):
                z_copy(way, r, s).wait_send()
                sib_copy(way, r, s).wait_send()
    for f in range(2):
        for way in range(2):
            for s in range(2):
                @pl.when(native)
                def _():
                    first_copy(f, way, home[f], s).wait_send()

            @pl.when(jnp.logical_not(native))
            def _():
                first_copy(f, way, near[f][way], way).wait_send()

            for o in range(2):
                relay_copy(f, way, o).wait_send()
                for s in range(2):
                    next_copy(f, way, o, s).wait_send()


    for j in range(8):
        device, mine = pc.owner(j)

        @pl.when(jnp.logical_not(mine))
        def _():
            plan_copy(0, j, device).wait_recv()

    listed = pltpu.make_async_copy(plan, todo, todo_sem)
    listed.start()
    listed.wait()

    @pl.when(k == 0)
    def _():
        for j in range(16):
            device, me = pc.meeter(j)

            @pl.when(jnp.logical_not(me))
            def _():
                plan_copy(j, z, device).wait_send()

    lane = lax.broadcasted_iota(jnp.int32, (256, 128), 1)
    contract = (((1,), (1,)), ((), ()))
    pot[...] = jnp.zeros(pot.shape, jnp.float32)
    found[...] = jnp.zeros(found.shape, jnp.float32)

    def log_sums(a, b, g_from, index_from):
        bias = jnp.sum(jnp.where(lane == index_from, turned[g_from], 0.0), axis=1, keepdims=True)
        score = lax.dot_general(a, b, contract, preferred_element_type=jnp.float32) * SCALE + bias
        peak = jnp.max(score, axis=0, keepdims=True)
        return peak + jnp.log2(jnp.sum(jnp.exp2(score - peak), axis=0, keepdims=True))

    for step in range(ITERS):
        turn = step % 2
        spread_wait(pc, level, table.at[turn], lv_send.at[turn], lv_recv.at[turn])
        for g in range(2):
            turned[g] = table[turn, 8 * g : 8 * g + 8].reshape(128, 256).T

        def line_of_pairs(a, carry):
            sums = []
            for d in range(8):
                code = jnp.maximum(todo[a, d, 0] - 1, 0)
                bs = code // 16
                bt = code % 16
                xs = src[a, bs]
                ys = tgt[d, bt]
                sums.append((log_sums(xs, ys, 0, a * 16 + bs), log_sums(ys, xs, 1, d * 16 + bt)))
            for d in range(8):
                down, across = sums[d]
                parts[8 + d, pl.ds(a, 1), :] = down
                parts[a, pl.ds(d, 1), :] = across
            return carry

        lax.fori_loop(0, 8, line_of_pairs, 0)

        def part_copy(j, slot, device):
            return remote(
                parts.at[j], gathered.at[turn, slot], part_send.at[turn, j], part_recv.at[turn, slot], device
            )

        for j in range(16):
            device, mine = pc.owner(j)
            slot = pc.meet_slot(j)

            @pl.when(jnp.logical_not(mine))
            def _():
                part_copy(j, slot, device).start()

            @pl.when(mine)
            def _():
                gathered[turn, slot] = parts[j]

        for j in range(16):
            device, me = pc.meeter(j)

            @pl.when(jnp.logical_not(me))
            def _():
                part_copy(j, j, device).wait_recv()

        block_of = (meet[...] + 15) // 16 - 1
        for half in range(2):
            cols = pl.ds(128 * half, 128)
            rows = gathered[turn, :, :, cols]
            for b in range(12):
                held = jnp.where(block_of == b, rows, EMPTY)
                peak = jnp.max(jnp.max(held, axis=0), axis=0, keepdims=True)
                mass = jnp.sum(jnp.sum(jnp.exp2(held - peak), axis=0), axis=0, keepdims=True)
                found[b : b + 1, cols] = peak + jnp.log2(mass)
        new_pot = 0.5 * (pot[...] + norm[...] - LN2 * found[...])
        pot[...] = new_pot
        if step < ITERS - 1:
            level[...] = LOG2E * (new_pot + weight[...] - norm[...])
            spread_start(pc, level, table.at[1 - turn], lv_send.at[1 - turn], lv_recv.at[1 - turn])
        for j in range(16):
            device, mine = pc.owner(j)

            @pl.when(jnp.logical_not(mine))
            def _():
                part_copy(j, j, device).wait_send()

    pot_out[...] = pot[0:12]


def per_device(embeds, log_weights, listing):
    emb = embeds[0]
    pairs = listing[0]
    sq = jnp.sum(jnp.square(emb.astype(jnp.float32)), axis=2)
    norm = jnp.pad(INV_BLUR * sq, ((0, 4), (0, 0)))
    weight = jnp.pad(log_weights[0], ((0, 4), (0, 0)))
    own_local = pairs[:, 0] % 12
    far_dev = pairs[:, 1] // 12
    far_local = pairs[:, 1] % 12
    fx = far_dev // 32
    fy = (far_dev // 8) % 4
    fz = far_dev % 8
    place_src = (fz * 2 + (fx + fy) % 2) * 8 + fy * 2 + fx // 2
    place_tgt = (fy * 4 + fx) * 8 + fz
    place = jnp.where(lax.axis_index("side") == 0, place_src, place_tgt)
    hot = place[:, None] == jnp.arange(128)[None, :]
    meet = jnp.sum(jnp.where(hot, (own_local * 16 + far_local + 1)[:, None], 0), axis=0)
    meet = jnp.broadcast_to(meet.reshape(16, 8, 1), (16, 8, 128))
    DMA = pltpu.SemaphoreType.DMA
    any_spec = pl.BlockSpec(memory_space=pl.ANY)
    vmem = pl.BlockSpec(memory_space=pltpu.VMEM)
    f32 = jnp.float32
    pot = pl.pallas_call(
        sinkhorn_kernel,
        out_shape=jax.ShapeDtypeStruct((12, 256), f32),
        in_specs=[any_spec, vmem, vmem, vmem],
        out_specs=vmem,
        scratch_shapes=[
            pltpu.VMEM((8, 12, 256, 256), jnp.bfloat16),
            pltpu.VMEM((8, 12, 256, 256), jnp.bfloat16),
            pltpu.VMEM((2, 16, 16, 256), f32),
            pltpu.VMEM((16, 256), f32),
            pltpu.VMEM((8, 8, 128), jnp.int32),
            pltpu.SMEM((8, 8, 128), jnp.int32),
            pltpu.VMEM((2, 256, 128), f32),
            pltpu.VMEM((16, 8, 256), f32),
            pltpu.VMEM((2, 16, 8, 256), f32),
            pltpu.VMEM((16, 256), f32),
            pltpu.VMEM((16, 256), f32),
            DMA,
            DMA((2, 2)),
            DMA((2, 2, 2)),
            DMA((2, 4, 2)),
            DMA((2, 4, 2)),
            DMA((2, 4, 2)),
            DMA((2, 4, 2)),
            DMA((2, 2, 2)),
            DMA((2, 2, 2)),
            DMA((2, 2, 2, 2)),
            DMA((2, 2, 2, 2)),
            DMA((2, 2, 2)),
            DMA((2, 2, 2)),
            DMA((16,)),
            DMA((8,)),
            DMA((2, 16)),
            DMA((2, 16)),
            DMA((2, 16)),
            DMA((2, 16)),
        ],
        compiler_params=pltpu.CompilerParams(collective_id=0, has_side_effects=True, vmem_limit_bytes=VMEM_CAP),
        name="sinkhorn",
    )(emb, meet, weight, norm)
    return pot[None]


def solution(mesh):
    placed = (
        P("side", ("group", "dev"), None, None),
        P("side", ("group", "dev"), None),
        P("side", ("group", "dev"), None),
    )
    return jax.shard_map(
        per_device,
        mesh=mesh,
        in_specs=placed,
        out_specs=P("side", ("group", "dev"), None),
        check_vma=False,
    )
```

```python
import math

import jax
import jax.numpy as jnp
from jax import lax
from jax.experimental import pallas as pl
from jax.experimental.pallas import tpu as pltpu
from jax.sharding import PartitionSpec as P

MESH = pl.DeviceIdType.MESH
ITERS = 3
MIDDLE = 3
NX, NY, NZ = 4, 4, 8
LOG2E = math.log2(math.e)
LN2 = math.log(2.0)
INV_BLUR = 10.0
SCALE = 2.0 * INV_BLUR * LOG2E
EMPTY = -1e30
VMEM_CAP = 50 * 1024 * 1024


def where(pred, a, b):
    return jnp.where(pred, a, b)


class Place:
    def __init__(self):
        self.k = lax.axis_index("side")
        self.x = lax.axis_index("group")
        dev = lax.axis_index("dev")
        self.y = dev // NZ
        self.z = dev % NZ
        self.kq = (self.x + self.y) % 2
        self.own_slot = self.y * 2 + self.x // 2

    def dev(self, k, x, y, z):
        return (k, x, y * NZ + z)

    def source_owner(self, a):
        return self.dev(jnp.int32(0), self.x, self.y, a), jnp.logical_and(self.k == 0, self.z == a)

    def target_owner(self, d):
        y0 = d // 2
        x0 = 2 * (d % 2) + (y0 + self.k) % 2
        me = jnp.logical_and(self.k == 1, jnp.logical_and(self.x == x0, self.y == y0))
        return self.dev(jnp.int32(1), x0, y0, self.z), me

    def owner(self, j):
        return self.source_owner(jnp.int32(j)) if j < 8 else self.target_owner(jnp.int32(j - 8))

    def meeter(self, j):
        src = self.k == 0
        kk = where(src, j % 2, self.kq)
        xx = where(src, self.x, j % 4)
        yy = where(src, self.y, j // 4)
        zz = where(src, j // 2, self.z)
        me = jnp.logical_and(
            jnp.logical_and(kk == self.k, xx == self.x), jnp.logical_and(yy == self.y, zz == self.z)
        )
        return self.dev(kk, xx, yy, zz), me

    def peers(self):
        return 16 - where(jnp.logical_or(self.k == 0, self.kq == 1), 1, 0)

    def level_slot(self):
        return where(self.k == 0, self.z, 8 + self.own_slot)

    def meet_slot(self, side):
        return self.z * 2 + self.k if side == 0 else self.y * 4 + self.x


def remote(src, dst, send_sem, recv_sem, device):
    return pltpu.make_async_remote_copy(
        src_ref=src, dst_ref=dst, send_sem=send_sem, recv_sem=recv_sem, device_id=device, device_id_type=MESH
    )


def spread_start(pc, level, table, send_sem, recv_sem):
    slot = pc.level_slot()
    for j in range(16):
        device, me = pc.meeter(j)

        @pl.when(jnp.logical_not(me))
        def _():
            remote(level, table.at[slot], send_sem.at[j], recv_sem.at[slot], device).start()

        @pl.when(me)
        def _():
            table[slot] = level[...]


def spread_landed(pc, level, table, send_sem, recv_sem, side):
    for j in range(8 * side, 8 * side + 8):
        owner, mine = pc.owner(j)

        @pl.when(jnp.logical_not(mine))
        def _():
            remote(level, table.at[j], send_sem.at[j], recv_sem.at[j], owner).wait_recv()


def spread_sent(pc, level, table, send_sem, recv_sem):
    for j in range(16):
        device, me = pc.meeter(j)

        @pl.when(jnp.logical_not(me))
        def _():
            remote(level, table.at[j], send_sem.at[j], recv_sem.at[j], device).wait_send()


def signal(sem, device):
    pl.semaphore_signal(sem, inc=1, device_id=device, device_id_type=MESH)


def sinkhorn_kernel(
    emb, meet, weight, pot_out,
    src, tgt, mine_blocks, norm, table, level, plan, todo, turned, parts, gathered, pot, found,
    todo_sem, norm_sem, local_sem, own_sem, z_out, first_out, next_out, z_send, z_recv, sib_send, sib_recv,
    first_send, first_recv, next_send, next_recv, relay_send, relay_recv,
    plan_send, plan_recv, lv_send, lv_recv, part_send, part_recv,
):
    pc = Place()
    k, x, y, z = pc.k, pc.x, pc.y, pc.z
    sibling = pc.dev(1 - k, x, y, z)
    zdev = [pc.dev(k, x, y, (z + 1) % NZ), pc.dev(k, x, y, (z + NZ - 1) % NZ)]
    xdev = [pc.dev(k, (x + 1) % NX, y, z), pc.dev(k, (x + NX - 1) % NX, y, z)]
    ydev = [pc.dev(k, x, (y + 1) % NY, z), pc.dev(k, x, (y + NY - 1) % NY, z)]

    barrier = pltpu.get_barrier_semaphore()
    for device in [sibling] + zdev + xdev + ydev:
        signal(barrier, device)
    for j in range(16):
        device, mine = pc.owner(j)

        @pl.when(jnp.logical_not(mine))
        def _():
            signal(barrier, device)

    pl.semaphore_wait(barrier, 7 + pc.peers())

    native = k == pc.kq

    def src_at(h, z0, s):
        return src.at[z0, pl.ds(6 * h + 3 * s, 3)]

    def tgt_at(f, line, o, s, core=k):
        if f == 0:
            return tgt.at[line * 2 + o, pl.ds(3 * s, 3)]
        return tgt.at[(2 * o + (line + core) % 2) * 2 + line // 2, pl.ds(6 + 3 * s, 3)]

    line_of = [y, x]
    spot_of = [x, y]
    spread_dev = [xdev, ydev]
    onward_dev = [ydev, xdev]

    own_line = pc.own_slot

    def z_first(way, h, s):
        part = emb.at[pl.ds(6 * h + 3 * s, 3)]
        z1 = (z + 1) % NZ if way == 0 else (z + NZ - 1) % NZ
        return remote(
            part, src_at(h, z, s), z_out.at[way, h, s], z_recv.at[way, 0, s], pc.dev(jnp.int32(h), x, y, z1)
        )

    def to_core(device):
        return (pc.kq,) + device[1:]

    def tgt_first(f, way, s):
        part = emb.at[pl.ds(6 * f + 3 * s, 3)]
        home_at = tgt.at[own_line, pl.ds(6 * f + 3 * s, 3)]
        return remote(part, home_at, first_out.at[f, way, s], first_recv.at[f, way, s], to_core(spread_dev[f][way]))

    def tgt_next(f, way, s):
        part = emb.at[pl.ds(6 * f + 3 * s, 3)]
        home_at = tgt.at[own_line, pl.ds(6 * f + 3 * s, 3)]
        return remote(
            part, home_at, next_out.at[f, way, s], next_recv.at[f, way, spot_of[f] // 2, s], to_core(onward_dev[f][way])
        )

    def norm_copy():
        return pltpu.make_async_copy(emb, mine_blocks, norm_sem)

    def src_local():
        return pltpu.make_async_copy(emb, src.at[z], local_sem)

    def src_sibling():
        return remote(emb, src.at[z], own_sem.at[0], own_sem.at[1], sibling)

    def tgt_local():
        return pltpu.make_async_copy(emb, tgt.at[own_line], local_sem)

    def tgt_sibling():
        return remote(emb, tgt.at[own_line], own_sem.at[0], own_sem.at[1], sibling)

    @pl.when(k == 0)
    def _():
        for s in range(2):
            for way in range(2):
                for h in range(2):
                    z_first(way, h, s).start()
        src_local().start()
        src_sibling().start()

    @pl.when(k == 1)
    def _():
        for s in range(2):
            for f in range(2):
                for way in range(2):
                    tgt_first(f, way, s).start()
        for s in range(2):
            for f in range(2):
                for way in range(2):
                    tgt_next(f, way, s).start()

        @pl.when(pc.kq == 1)
        def _():
            tgt_local().start()

        @pl.when(pc.kq == 0)
        def _():
            tgt_sibling().start()

    norm_copy().start()
    norm_copy().wait()
    ones = jnp.ones((8, 256), jnp.bfloat16)
    norm[...] = jnp.zeros(norm.shape, jnp.float32)
    level[...] = jnp.zeros(level.shape, jnp.float32)

    def norm_of(b, carry):
        value = mine_blocks[b].astype(jnp.float32)
        square = value * value
        high = square.astype(jnp.bfloat16)
        low = (square - high.astype(jnp.float32)).astype(jnp.bfloat16)
        across = (((1,), (1,)), ((), ()))
        total = lax.dot_general(ones, high, across, preferred_element_type=jnp.float32)
        total = total + lax.dot_general(ones, low, across, preferred_element_type=jnp.float32)
        norm[pl.ds(b, 1), :] = INV_BLUR * total[0:1]
        return carry

    lax.fori_loop(0, 12, norm_of, 0)
    level[0:12] = LOG2E * (weight[...] - norm[0:12])
    spread_start(pc, level, table.at[0], lv_send.at[0], lv_recv.at[0])

    def plan_copy(j, slot, device):
        return remote(meet.at[j], plan.at[slot], plan_send.at[j], plan_recv.at[slot], device)

    @pl.when(k == 0)
    def _():
        for j in range(16):
            device, me = pc.meeter(j)

            @pl.when(jnp.logical_not(me))
            def _():
                plan_copy(j, z, device).start()

            @pl.when(me)
            def _():
                plan[z] = meet[j]

    def z_copy(way, r, s):
        z0 = (z - r + NZ) % NZ if way == 0 else (z + r) % NZ
        part = src.at[z0, pl.ds(6 * k + 3 * s, 3)]
        return remote(part, part, z_send.at[way, r, s], z_recv.at[way, r, s], zdev[way])

    def z_landed(way, r, s):
        z0 = (z - r - 1 + NZ) % NZ if way == 0 else (z + r + 1) % NZ
        part = src.at[z0, pl.ds(6 * k + 3 * s, 3)]
        return remote(part, part, z_send.at[way, r, s], z_recv.at[way, r, s], zdev[way])

    def sib_copy(way, r, s):
        z0 = (z - r - 1 + NZ) % NZ if way == 0 else (z + r + 1) % NZ
        part = src.at[z0, pl.ds(6 * k + 3 * s, 3)]
        return remote(part, part, sib_send.at[way, r, s], sib_recv.at[way, r, s], sibling)

    def sib_landed(way, r, s):
        z0 = (z - r - 1 + NZ) % NZ if way == 0 else (z + r + 1) % NZ
        part = src.at[z0, pl.ds(6 * (1 - k) + 3 * s, 3)]
        return remote(part, part, sib_send.at[way, r, s], sib_recv.at[way, r, s], sibling)

    def z_subs(way, r):
        return (0, 1) if r < 3 else (way,)

    def first_copy(f, way, o, s):
        part = tgt_at(f, line_of[f], o, s)
        return remote(part, part, first_send.at[f, way, s], first_recv.at[f, way, s], spread_dev[f][way])

    def next_copy(f, way, o, s):
        part = tgt_at(f, line_of[f], o, s)
        return remote(part, part, next_send.at[f, way, o, s], next_recv.at[f, way, o, s], onward_dev[f][way])

    def from_line(f, way):
        n = line_of[f]
        return (n + 3) % 4 if way == 0 else (n + 1) % 4

    def next_landed(f, way, o, s):
        part = tgt_at(f, from_line(f, way), o, s)
        return remote(part, part, next_send.at[f, way, o, s], next_recv.at[f, way, o, s], onward_dev[f][way])

    def relay_copy(f, way, o):
        part = tgt_at(f, from_line(f, way), o, way)
        return remote(part, part, relay_send.at[f, way, o], relay_recv.at[f, way, o], onward_dev[f][way])

    def relay_landed(f, way, o):
        part = tgt_at(f, (line_of[f] + 2) % 4, o, way)
        return remote(part, part, relay_send.at[f, way, o], relay_recv.at[f, way, o], onward_dev[f][way])

    home = [spot_of[f] // 2 for f in range(2)]
    near = [[((spot_of[f] + 3) % 4) // 2, ((spot_of[f] + 1) % 4) // 2] for f in range(2)]

    def z_forward(r):
        for s in range(2):
            for way in range(2):
                if s in z_subs(way, r):
                    z_landed(way, r, s).wait_recv()
                    if r < 3 and s in z_subs(way, r + 1):
                        z_copy(way, r + 1, s).start()
                    sib_copy(way, r, s).start()

    z_forward(0)

    @pl.when(jnp.logical_not(native))
    def _():
        for s in range(2):
            for f in range(2):
                for way in range(2):
                    o = near[f][way]
                    first_copy(f, way, o, s).wait_recv()
                    if s == way:
                        first_copy(f, way, o, s).start()
                    for w in range(2):
                        next_copy(f, w, o, s).start()

    z_forward(1)

    @pl.when(native)
    def _():
        for f in range(2):
            for way in range(2):
                o = 1 - home[f]
                first_copy(f, way, o, way).wait_recv()
                for w in range(2):
                    next_copy(f, w, o, way).start()

    def onward(nth):
        for s in range(2):
            for f in range(2):
                o = home[f] if nth == 0 else 1 - home[f]
                for way in range(2):
                    next_landed(f, way, o, s).wait_recv()
                    if s == way:
                        relay_copy(f, way, o).start()

    onward(0)
    z_forward(2)
    onward(1)
    z_forward(3)

    for f in range(2):
        for way in range(2):
            for o in range(2):
                relay_landed(f, way, o).wait_recv()
    for r in range(4):
        for way in range(2):
            for s in z_subs(way, r):
                sib_landed(way, r, s).wait_recv()

    @pl.when(k == 0)
    def _():
        src_local().wait()
        src_sibling().wait_send()
        for s in range(2):
            for way in range(2):
                for h in range(2):
                    z_first(way, h, s).wait_send()

        @pl.when(pc.kq == 0)
        def _():
            tgt_sibling().wait_recv()

    @pl.when(k == 1)
    def _():
        src_sibling().wait_recv()

        @pl.when(pc.kq == 1)
        def _():
            tgt_local().wait()

        @pl.when(pc.kq == 0)
        def _():
            tgt_sibling().wait_send()

        for s in range(2):
            for f in range(2):
                for way in range(2):
                    tgt_first(f, way, s).wait_send()
                    tgt_next(f, way, s).wait_send()

    for r in range(4):
        for way in range(2):
            for s in z_subs(way, r):
                if r > 0:
                    z_copy(way, r, s).wait_send()
                sib_copy(way, r, s).wait_send()
    for f in range(2):
        for way in range(2):
            for o in range(2):
                relay_copy(f, way, o).wait_send()

            @pl.when(native)
            def _():
                next_copy(f, way, 1 - home[f], 0).wait_send()
                next_copy(f, way, 1 - home[f], 1).wait_send()

            @pl.when(jnp.logical_not(native))
            def _():
                first_copy(f, way, near[f][way], way).wait_send()
                for o in range(2):
                    for s in range(2):
                        next_copy(f, way, o, s).wait_send()

    for j in range(8):
        device, mine = pc.owner(j)

        @pl.when(jnp.logical_not(mine))
        def _():
            plan_copy(0, j, device).wait_recv()

    listed = pltpu.make_async_copy(plan, todo, todo_sem)
    listed.start()
    listed.wait()

    @pl.when(k == 0)
    def _():
        for j in range(16):
            device, me = pc.meeter(j)

            @pl.when(jnp.logical_not(me))
            def _():
                plan_copy(j, z, device).wait_send()

    lane = lax.broadcasted_iota(jnp.int32, (256, 128), 1)
    contract = (((1,), (1,)), ((), ()))
    pot[...] = jnp.zeros(pot.shape, jnp.float32)
    found[...] = jnp.zeros(found.shape, jnp.float32)

    def log_sums(a, b, g_from, index_from):
        bias = jnp.sum(jnp.where(lane == index_from, turned[g_from], 0.0), axis=1, keepdims=True)
        score = lax.dot_general(a, b, contract, preferred_element_type=jnp.float32) * SCALE + bias
        peak = jnp.max(score, axis=0, keepdims=True)
        return peak + jnp.log2(jnp.sum(jnp.exp2(score - peak), axis=0, keepdims=True))

    def level_copies(turn):
        return (pc, level, table.at[turn], lv_send.at[turn], lv_recv.at[turn])

    def take_levels(side, step):
        spread_landed(*level_copies(step % 2), side)
        turned[side] = table[step % 2, 8 * side : 8 * side + 8].reshape(128, 256).T

    def part_copy(side, step, i, slot, device):
        turn = step % 2
        return remote(
            parts.at[8 * side + i], gathered.at[turn, slot], part_send.at[turn, 8 * side + i], part_recv.at[turn, slot],
            device,
        )

    def sums_of(side, step):
        def body(i, carry):
            sums = []
            for u in range(8):
                a, d = (i, u) if side == 0 else (u, i)
                code = jnp.maximum(todo[a, d, 0] - 1, 0)
                bs = code // 16
                bt = code % 16
                xs = src[a, bs]
                ys = tgt[d, bt]
                if side == 0:
                    sums.append(log_sums(ys, xs, 1, d * 16 + bt))
                else:
                    sums.append(log_sums(xs, ys, 0, a * 16 + bs))
            for u in range(8):
                parts[8 * side + i, u : u + 1, :] = sums[u]
            device, mine = pc.source_owner(i) if side == 0 else pc.target_owner(i)
            slot = pc.meet_slot(side)

            @pl.when(jnp.logical_not(mine))
            def _():
                part_copy(side, step, i, slot, device).start()

            @pl.when(mine)
            def _():
                gathered[step % 2, slot] = parts[8 * side + i]

            return carry

        return body

    def parts_sent(side, step):
        for j in range(8):
            device, mine = pc.owner(8 * side + j)

            @pl.when(jnp.logical_not(mine))
            def _():
                part_copy(side, step, j, 0, device).wait_send()

    def combine(step):
        turn = step % 2
        for j in range(16):
            device, me = pc.meeter(j)

            @pl.when(jnp.logical_not(me))
            def _():
                part_copy(0, step, 0, j, device).wait_recv()

        block_of = (meet[...] + 15) // 16 - 1
        for half in range(2):
            cols = pl.ds(128 * half, 128)
            rows = gathered[turn, :, :, cols]
            for b in range(12):
                held = jnp.where(block_of == b, rows, EMPTY)
                peak = jnp.max(jnp.max(held, axis=0), axis=0, keepdims=True)
                mass = jnp.sum(jnp.sum(jnp.exp2(held - peak), axis=0), axis=0, keepdims=True)
                found[b : b + 1, cols] = peak + jnp.log2(mass)
        new_pot = 0.5 * (pot[...] + norm[...] - LN2 * found[...])
        pot[...] = new_pot
        if step < ITERS - 1:
            spread_sent(*level_copies(turn))
            level[0:12] = LOG2E * (new_pot[0:12] + weight[...] - norm[0:12])
            spread_start(*level_copies(1 - turn))

    order = []
    for step in range(ITERS):
        order += [(0, step), (1, step)] if step % 2 == 0 else [(1, step), (0, step)]
    for n, (side, step) in enumerate(order):
        take_levels(1 - side, step)
        if step > 0:
            parts_sent(side, step - 1)
        body = sums_of(side, step)
        if n == 0:
            lax.fori_loop(0, 8, body, 0)
        else:
            lax.fori_loop(0, MIDDLE, body, 0)
            last_side, last_step = order[n - 1]

            @pl.when(k == last_side)
            def _():
                combine(last_step)

            lax.fori_loop(MIDDLE, 8, body, 0)
    last_side, last_step = order[-1]

    @pl.when(k == last_side)
    def _():
        combine(last_step)

    for side in range(2):
        parts_sent(side, ITERS - 1)
    spread_sent(*level_copies((ITERS - 1) % 2))
    pot_out[...] = pot[0:12]


def per_device(embeds, log_weights, listing):
    emb = embeds[0]
    pairs = listing[0]
    own_local = pairs[:, 0] % 12
    far_dev = pairs[:, 1] // 12
    far_local = pairs[:, 1] % 12
    fx = far_dev // 32
    fy = (far_dev // 8) % 4
    fz = far_dev % 8
    place_src = (fz * 2 + (fx + fy) % 2) * 8 + fy * 2 + fx // 2
    place_tgt = (fy * 4 + fx) * 8 + fz
    place = jnp.where(lax.axis_index("side") == 0, place_src, place_tgt)
    hot = place[:, None] == jnp.arange(128)[None, :]
    meet = jnp.sum(jnp.where(hot, (own_local * 16 + far_local + 1)[:, None], 0), axis=0)
    meet = jnp.broadcast_to(meet.reshape(16, 8, 1), (16, 8, 128))
    DMA = pltpu.SemaphoreType.DMA
    any_spec = pl.BlockSpec(memory_space=pl.ANY)
    vmem = pl.BlockSpec(memory_space=pltpu.VMEM)
    f32 = jnp.float32
    pot = pl.pallas_call(
        sinkhorn_kernel,
        out_shape=jax.ShapeDtypeStruct((12, 256), f32),
        in_specs=[any_spec, vmem, vmem],
        out_specs=vmem,
        scratch_shapes=[
            pltpu.VMEM((8, 12, 256, 256), jnp.bfloat16),
            pltpu.VMEM((8, 12, 256, 256), jnp.bfloat16),
            pltpu.VMEM((12, 256, 256), jnp.bfloat16),
            pltpu.VMEM((16, 256), f32),
            pltpu.VMEM((2, 16, 16, 256), f32),
            pltpu.VMEM((16, 256), f32),
            pltpu.VMEM((8, 8, 128), jnp.int32),
            pltpu.SMEM((8, 8, 128), jnp.int32),
            pltpu.VMEM((2, 256, 128), f32),
            pltpu.VMEM((16, 8, 256), f32),
            pltpu.VMEM((2, 16, 8, 256), f32),
            pltpu.VMEM((16, 256), f32),
            pltpu.VMEM((16, 256), f32),
            DMA,
            DMA,
            DMA,
            DMA((2,)),
            DMA((2, 2, 2)),
            DMA((2, 2, 2)),
            DMA((2, 2, 2)),
            DMA((2, 4, 2)),
            DMA((2, 4, 2)),
            DMA((2, 4, 2)),
            DMA((2, 4, 2)),
            DMA((2, 2, 2)),
            DMA((2, 2, 2)),
            DMA((2, 2, 2, 2)),
            DMA((2, 2, 2, 2)),
            DMA((2, 2, 2)),
            DMA((2, 2, 2)),
            DMA((16,)),
            DMA((8,)),
            DMA((2, 16)),
            DMA((2, 16)),
            DMA((2, 16)),
            DMA((2, 16)),
        ],
        compiler_params=pltpu.CompilerParams(collective_id=0, has_side_effects=True, vmem_limit_bytes=VMEM_CAP),
        name="sinkhorn",
    )(emb, meet, log_weights[0])
    return pot[None]


def solution(mesh):
    placed = (
        P("side", ("group", "dev"), None, None),
        P("side", ("group", "dev"), None),
        P("side", ("group", "dev"), None),
    )
    return jax.shard_map(
        per_device,
        mesh=mesh,
        in_specs=placed,
        out_specs=P("side", ("group", "dev"), None),
        check_vma=False,
    )
```

```python
import math

import jax
import jax.numpy as jnp
from jax import lax
from jax.experimental import pallas as pl
from jax.experimental.pallas import tpu as pltpu
from jax.sharding import PartitionSpec as P

MESH = pl.DeviceIdType.MESH
ITERS = 3
LATE = 3
NX, NY, NZ = 4, 4, 8
LOG2E = math.log2(math.e)
LN2 = math.log(2.0)
INV_BLUR = 10.0
SCALE = 2.0 * INV_BLUR * LOG2E
EMPTY = -1e30
VMEM_CAP = 50 * 1024 * 1024


def where(pred, a, b):
    return jnp.where(pred, a, b)


class Place:
    def __init__(self):
        self.k = lax.axis_index("side")
        self.x = lax.axis_index("group")
        dev = lax.axis_index("dev")
        self.y = dev // NZ
        self.z = dev % NZ
        self.kq = (self.x + self.y) % 2
        self.own_slot = self.y * 2 + self.x // 2

    def dev(self, k, x, y, z):
        return (k, x, y * NZ + z)

    def source_owner(self, a):
        return self.dev(jnp.int32(0), self.x, self.y, a), jnp.logical_and(self.k == 0, self.z == a)

    def target_owner(self, d):
        y0 = d // 2
        x0 = 2 * (d % 2) + (y0 + self.k) % 2
        me = jnp.logical_and(self.k == 1, jnp.logical_and(self.x == x0, self.y == y0))
        return self.dev(jnp.int32(1), x0, y0, self.z), me

    def owner(self, j):
        return self.source_owner(jnp.int32(j)) if j < 8 else self.target_owner(jnp.int32(j - 8))

    def meeter(self, j):
        src = self.k == 0
        kk = where(src, j % 2, self.kq)
        xx = where(src, self.x, j % 4)
        yy = where(src, self.y, j // 4)
        zz = where(src, j // 2, self.z)
        me = jnp.logical_and(
            jnp.logical_and(kk == self.k, xx == self.x), jnp.logical_and(yy == self.y, zz == self.z)
        )
        return self.dev(kk, xx, yy, zz), me

    def peers(self):
        return 16 - where(jnp.logical_or(self.k == 0, self.kq == 1), 1, 0)

    def level_slot(self):
        return where(self.k == 0, self.z, 8 + self.own_slot)

    def meet_slot(self, side):
        return self.z * 2 + self.k if side == 0 else self.y * 4 + self.x


def remote(src, dst, send_sem, recv_sem, device):
    return pltpu.make_async_remote_copy(
        src_ref=src, dst_ref=dst, send_sem=send_sem, recv_sem=recv_sem, device_id=device, device_id_type=MESH
    )


def spread_start(pc, level, table, send_sem, recv_sem):
    slot = pc.level_slot()
    for j in range(16):
        device, me = pc.meeter(j)

        @pl.when(jnp.logical_not(me))
        def _():
            remote(level, table.at[slot], send_sem.at[j], recv_sem.at[slot], device).start()

        @pl.when(me)
        def _():
            table[slot] = level[...]


def spread_landed(pc, level, table, send_sem, recv_sem, side):
    for j in range(8 * side, 8 * side + 8):
        owner, mine = pc.owner(j)

        @pl.when(jnp.logical_not(mine))
        def _():
            remote(level, table.at[j], send_sem.at[j], recv_sem.at[j], owner).wait_recv()


def spread_sent(pc, level, table, send_sem, recv_sem):
    for j in range(16):
        device, me = pc.meeter(j)

        @pl.when(jnp.logical_not(me))
        def _():
            remote(level, table.at[j], send_sem.at[j], recv_sem.at[j], device).wait_send()


def signal(sem, device):
    pl.semaphore_signal(sem, inc=1, device_id=device, device_id_type=MESH)


def sinkhorn_kernel(
    emb, pairs, weights, pot_out,
    src, tgt, meet, weight, mine_blocks, norm, table, level, plan, todo, turned, turned_one, parts, gathered, pot, found,
    todo_sem, norm_sem, weight_sem, local_sem, own_sem, z_out, first_out, next_out, z_send, z_recv, sib_send, sib_recv,
    first_send, first_recv, next_send, next_recv, relay_send, relay_recv,
    plan_send, plan_recv, lv_send, lv_recv, part_send, part_recv,
):
    pc = Place()
    k, x, y, z = pc.k, pc.x, pc.y, pc.z
    sibling = pc.dev(1 - k, x, y, z)
    zdev = [pc.dev(k, x, y, (z + 1) % NZ), pc.dev(k, x, y, (z + NZ - 1) % NZ)]
    xdev = [pc.dev(k, (x + 1) % NX, y, z), pc.dev(k, (x + NX - 1) % NX, y, z)]
    ydev = [pc.dev(k, x, (y + 1) % NY, z), pc.dev(k, x, (y + NY - 1) % NY, z)]

    barrier = pltpu.get_barrier_semaphore()
    for device in [sibling] + zdev + xdev + ydev:
        signal(barrier, device)
    for j in range(16):
        device, mine = pc.owner(j)

        @pl.when(jnp.logical_not(mine))
        def _():
            signal(barrier, device)

    pl.semaphore_wait(barrier, 7 + pc.peers())

    native = k == pc.kq

    def src_at(h, z0, s):
        return src.at[z0, pl.ds(6 * h + 3 * s, 3)]

    def tgt_at(f, line, o, s, core=k):
        if f == 0:
            return tgt.at[line * 2 + o, pl.ds(3 * s, 3)]
        return tgt.at[(2 * o + (line + core) % 2) * 2 + line // 2, pl.ds(6 + 3 * s, 3)]

    line_of = [y, x]
    spot_of = [x, y]
    spread_dev = [xdev, ydev]
    onward_dev = [ydev, xdev]

    own_line = pc.own_slot

    def z_first(way, h, s):
        part = emb.at[pl.ds(6 * h + 3 * s, 3)]
        z1 = (z + 1) % NZ if way == 0 else (z + NZ - 1) % NZ
        return remote(
            part, src_at(h, z, s), z_out.at[way, h, s], z_recv.at[way, 0, s], pc.dev(jnp.int32(h), x, y, z1)
        )

    def to_core(device):
        return (pc.kq,) + device[1:]

    def tgt_first(f, way, s):
        part = emb.at[pl.ds(6 * f + 3 * s, 3)]
        home_at = tgt.at[own_line, pl.ds(6 * f + 3 * s, 3)]
        return remote(part, home_at, first_out.at[f, way, s], first_recv.at[f, way, s], to_core(spread_dev[f][way]))

    def tgt_next(f, way, s):
        part = emb.at[pl.ds(6 * f + 3 * s, 3)]
        home_at = tgt.at[own_line, pl.ds(6 * f + 3 * s, 3)]
        return remote(
            part, home_at, next_out.at[f, way, s], next_recv.at[f, way, spot_of[f] // 2, s], to_core(onward_dev[f][way])
        )

    def norm_copy():
        return pltpu.make_async_copy(emb, mine_blocks, norm_sem)

    def src_local():
        return pltpu.make_async_copy(emb, src.at[z], local_sem)

    def src_sibling():
        return remote(emb, src.at[z], own_sem.at[0], own_sem.at[1], sibling)

    def tgt_local():
        return pltpu.make_async_copy(emb, tgt.at[own_line], local_sem)

    def tgt_sibling():
        return remote(emb, tgt.at[own_line], own_sem.at[0], own_sem.at[1], sibling)

    @pl.when(k == 0)
    def _():
        for s in range(2):
            for way in range(2):
                for h in range(2):
                    z_first(way, h, s).start()
        src_local().start()
        src_sibling().start()

    @pl.when(k == 1)
    def _():
        for s in range(2):
            for f in range(2):
                for way in range(2):
                    tgt_first(f, way, s).start()
        for s in range(2):
            for f in range(2):
                for way in range(2):
                    tgt_next(f, way, s).start()

        @pl.when(pc.kq == 1)
        def _():
            tgt_local().start()

        @pl.when(pc.kq == 0)
        def _():
            tgt_sibling().start()

    norm_copy().start()
    weight_copy = pltpu.make_async_copy(weights, weight, weight_sem)
    weight_copy.start()

    own_local = pairs[:, 0:1] - 12 * (x * 32 + y * 8 + z)
    far = pairs[:, 1:2]
    far_dev = (far * 43691) >> 19
    far_local = far - 12 * far_dev
    fx = far_dev >> 5
    fy = (far_dev >> 3) & 3
    fz = far_dev & 7
    place_src = (fz * 2 + ((fx + fy) & 1)) * 8 + fy * 2 + (fx >> 1)
    place_tgt = (fy * 4 + fx) * 8 + fz
    place = jnp.where(k == 0, place_src, place_tgt)
    hot = place == lax.broadcasted_iota(jnp.int32, (60, 128), 1)
    line = jnp.sum(jnp.where(hot, own_local * 16 + far_local + 1, 0), axis=0, keepdims=True)
    meet[...] = jnp.broadcast_to(line, (128, 128)).T.reshape(16, 8, 128)
    weight_copy.wait()
    norm_copy().wait()
    ones = jnp.ones((8, 256), jnp.bfloat16)
    norm[...] = jnp.zeros(norm.shape, jnp.float32)
    level[...] = jnp.zeros(level.shape, jnp.float32)

    def norm_of(b, carry):
        value = mine_blocks[b].astype(jnp.float32)
        square = value * value
        high = square.astype(jnp.bfloat16)
        low = (square - high.astype(jnp.float32)).astype(jnp.bfloat16)
        across = (((1,), (1,)), ((), ()))
        total = lax.dot_general(ones, high, across, preferred_element_type=jnp.float32)
        total = total + lax.dot_general(ones, low, across, preferred_element_type=jnp.float32)
        norm[pl.ds(b, 1), :] = INV_BLUR * total[0:1]
        return carry

    lax.fori_loop(0, 12, norm_of, 0)
    level[0:12] = LOG2E * (weight[...] - norm[0:12])
    spread_start(pc, level, table.at[0], lv_send.at[0], lv_recv.at[0])

    def plan_copy(j, slot, device):
        return remote(meet.at[j], plan.at[slot], plan_send.at[j], plan_recv.at[slot], device)

    @pl.when(k == 0)
    def _():
        for j in range(16):
            device, me = pc.meeter(j)

            @pl.when(jnp.logical_not(me))
            def _():
                plan_copy(j, z, device).start()

            @pl.when(me)
            def _():
                plan[z] = meet[j]

    def z_copy(way, r, s):
        z0 = (z - r + NZ) % NZ if way == 0 else (z + r) % NZ
        part = src.at[z0, pl.ds(6 * k + 3 * s, 3)]
        return remote(part, part, z_send.at[way, r, s], z_recv.at[way, r, s], zdev[way])

    def z_landed(way, r, s):
        z0 = (z - r - 1 + NZ) % NZ if way == 0 else (z + r + 1) % NZ
        part = src.at[z0, pl.ds(6 * k + 3 * s, 3)]
        return remote(part, part, z_send.at[way, r, s], z_recv.at[way, r, s], zdev[way])

    def sib_copy(way, r, s):
        z0 = (z - r - 1 + NZ) % NZ if way == 0 else (z + r + 1) % NZ
        part = src.at[z0, pl.ds(6 * k + 3 * s, 3)]
        return remote(part, part, sib_send.at[way, r, s], sib_recv.at[way, r, s], sibling)

    def sib_landed(way, r, s):
        z0 = (z - r - 1 + NZ) % NZ if way == 0 else (z + r + 1) % NZ
        part = src.at[z0, pl.ds(6 * (1 - k) + 3 * s, 3)]
        return remote(part, part, sib_send.at[way, r, s], sib_recv.at[way, r, s], sibling)

    def z_subs(way, r):
        return (0, 1) if r < 3 else (way,)

    def first_copy(f, way, o, s):
        part = tgt_at(f, line_of[f], o, s)
        return remote(part, part, first_send.at[f, way, s], first_recv.at[f, way, s], spread_dev[f][way])

    def next_copy(f, way, o, s):
        part = tgt_at(f, line_of[f], o, s)
        return remote(part, part, next_send.at[f, way, o, s], next_recv.at[f, way, o, s], onward_dev[f][way])

    def from_line(f, way):
        n = line_of[f]
        return (n + 3) % 4 if way == 0 else (n + 1) % 4

    def next_landed(f, way, o, s):
        part = tgt_at(f, from_line(f, way), o, s)
        return remote(part, part, next_send.at[f, way, o, s], next_recv.at[f, way, o, s], onward_dev[f][way])

    def relay_copy(f, way, o):
        part = tgt_at(f, from_line(f, way), o, way)
        return remote(part, part, relay_send.at[f, way, o], relay_recv.at[f, way, o], onward_dev[f][way])

    def relay_landed(f, way, o):
        part = tgt_at(f, (line_of[f] + 2) % 4, o, way)
        return remote(part, part, relay_send.at[f, way, o], relay_recv.at[f, way, o], onward_dev[f][way])

    home = [spot_of[f] // 2 for f in range(2)]
    near = [[((spot_of[f] + 3) % 4) // 2, ((spot_of[f] + 1) % 4) // 2] for f in range(2)]

    def z_forward(r):
        for s in range(2):
            for way in range(2):
                if s in z_subs(way, r):
                    z_landed(way, r, s).wait_recv()
                    if r < 3 and s in z_subs(way, r + 1):
                        z_copy(way, r + 1, s).start()
                    sib_copy(way, r, s).start()

    z_forward(0)

    @pl.when(jnp.logical_not(native))
    def _():
        for s in range(2):
            for f in range(2):
                for way in range(2):
                    o = near[f][way]
                    first_copy(f, way, o, s).wait_recv()
                    if s == way:
                        first_copy(f, way, o, s).start()
                    for w in range(2):
                        next_copy(f, w, o, s).start()

    z_forward(1)

    @pl.when(native)
    def _():
        for f in range(2):
            for way in range(2):
                o = 1 - home[f]
                first_copy(f, way, o, way).wait_recv()
                for w in range(2):
                    next_copy(f, w, o, way).start()

    def onward(nth):
        for s in range(2):
            for f in range(2):
                o = home[f] if nth == 0 else 1 - home[f]
                for way in range(2):
                    next_landed(f, way, o, s).wait_recv()
                    if s == way:
                        relay_copy(f, way, o).start()

    onward(0)
    z_forward(2)
    onward(1)
    z_forward(3)

    for f in range(2):
        for way in range(2):
            for o in range(2):
                relay_landed(f, way, o).wait_recv()
    for r in range(4):
        for way in range(2):
            for s in z_subs(way, r):
                sib_landed(way, r, s).wait_recv()

    @pl.when(k == 0)
    def _():
        src_local().wait()
        src_sibling().wait_send()
        for s in range(2):
            for way in range(2):
                for h in range(2):
                    z_first(way, h, s).wait_send()

        @pl.when(pc.kq == 0)
        def _():
            tgt_sibling().wait_recv()

    @pl.when(k == 1)
    def _():
        src_sibling().wait_recv()

        @pl.when(pc.kq == 1)
        def _():
            tgt_local().wait()

        @pl.when(pc.kq == 0)
        def _():
            tgt_sibling().wait_send()

        for s in range(2):
            for f in range(2):
                for way in range(2):
                    tgt_first(f, way, s).wait_send()
                    tgt_next(f, way, s).wait_send()

    for r in range(4):
        for way in range(2):
            for s in z_subs(way, r):
                if r > 0:
                    z_copy(way, r, s).wait_send()
                sib_copy(way, r, s).wait_send()
    for f in range(2):
        for way in range(2):
            for o in range(2):
                relay_copy(f, way, o).wait_send()

            @pl.when(native)
            def _():
                next_copy(f, way, 1 - home[f], 0).wait_send()
                next_copy(f, way, 1 - home[f], 1).wait_send()

            @pl.when(jnp.logical_not(native))
            def _():
                first_copy(f, way, near[f][way], way).wait_send()
                for o in range(2):
                    for s in range(2):
                        next_copy(f, way, o, s).wait_send()

    for j in range(8):
        device, mine = pc.owner(j)

        @pl.when(jnp.logical_not(mine))
        def _():
            plan_copy(0, j, device).wait_recv()

    listed = pltpu.make_async_copy(plan, todo, todo_sem)
    listed.start()
    listed.wait()

    @pl.when(k == 0)
    def _():
        for j in range(16):
            device, me = pc.meeter(j)

            @pl.when(jnp.logical_not(me))
            def _():
                plan_copy(j, z, device).wait_send()

    lane = lax.broadcasted_iota(jnp.int32, (256, 128), 1)
    contract = (((1,), (1,)), ((), ()))
    pot[...] = jnp.zeros(pot.shape, jnp.float32)
    found[...] = jnp.zeros(found.shape, jnp.float32)

    lane16 = lax.broadcasted_iota(jnp.int32, (256, 16), 1)

    def log_sums(a, b, bias):
        score = lax.dot_general(a, b, contract, preferred_element_type=jnp.float32) * SCALE + bias
        peak = jnp.max(score, axis=0, keepdims=True)
        return peak + jnp.log2(jnp.sum(jnp.exp2(score - peak), axis=0, keepdims=True))

    def level_copies(turn):
        return (pc, level, table.at[turn], lv_send.at[turn], lv_recv.at[turn])

    def take_levels(side, step):
        spread_landed(*level_copies(step % 2), side)
        turned[side] = table[step % 2, 8 * side : 8 * side + 8].reshape(128, 256).T

    def part_copy(side, step, i, slot, device):
        turn = step % 2
        return remote(
            parts.at[8 * side + i], gathered.at[turn, slot], part_send.at[turn, 8 * side + i], part_recv.at[turn, slot],
            device,
        )

    def part_out(side, step, i):
        device, mine = pc.source_owner(i) if side == 0 else pc.target_owner(i)
        slot = pc.meet_slot(side)

        @pl.when(jnp.logical_not(mine))
        def _():
            part_copy(side, step, i, slot, device).start()

        @pl.when(mine)
        def _():
            gathered[step % 2, slot] = parts[8 * side + i]

    def sums_of(side, step, outer, staged=False, before=None):
        def body(pair, carry):
            if before is not None:
                before(pair)
            if staged:
                for w in range(2):
                    i = pair * 2 + w
                    owner, mine = pc.source_owner(i) if outer == 0 else pc.target_owner(i)
                    _, _, rows, sent, landed = level_copies(step % 2)
                    j = 8 * outer + i

                    @pl.when(jnp.logical_not(mine))
                    def _():
                        remote(level, rows.at[j], sent.at[j], landed.at[j], owner).wait_recv()

                for w in range(2):
                    turned_one[w] = table[step % 2, 8 * outer + pair * 2 + w].T
            sums = []
            for w in range(2):
                i = pair * 2 + w
                for u in range(8):
                    a, d = (i, u) if outer == 0 else (u, i)
                    code = jnp.maximum(todo[a, d, 0] - 1, 0)
                    bs = code // 16
                    bt = code % 16
                    xs = src[a, bs]
                    ys = tgt[d, bt]
                    if side == 0:
                        left, right, row, base = ys, xs, bt, d
                    else:
                        left, right, row, base = xs, ys, bs, a
                    if staged:
                        bias = jnp.sum(jnp.where(lane16 == row, turned_one[w], 0.0), axis=1, keepdims=True)
                    else:
                        bias = jnp.sum(jnp.where(lane == base * 16 + row, turned[1 - side], 0.0), axis=1, keepdims=True)
                    sums.append(log_sums(left, right, bias))
            for w in range(2):
                i = pair * 2 + w
                for u in range(8):
                    if outer == side:
                        parts[8 * side + i, u : u + 1, :] = sums[8 * w + u]
                    else:
                        parts[8 * side + u, pl.ds(i, 1), :] = sums[8 * w + u]
            if outer == side:
                for w in range(2):
                    part_out(side, step, pair * 2 + w)
            return carry

        lax.fori_loop(0, 4, body, 0)
        if outer != side:
            for i in range(8):
                part_out(side, step, jnp.int32(i))

    def parts_sent(side, step):
        for j in range(8):
            device, mine = pc.owner(8 * side + j)

            @pl.when(jnp.logical_not(mine))
            def _():
                part_copy(side, step, j, 0, device).wait_send()

    def combine(step):
        turn = step % 2
        for j in range(16):
            device, me = pc.meeter(j)

            @pl.when(jnp.logical_not(me))
            def _():
                part_copy(0, step, 0, j, device).wait_recv()

        block_of = (meet[...] + 15) // 16 - 1
        for half in range(2):
            cols = pl.ds(128 * half, 128)
            rows = gathered[turn, :, :, cols]
            for b in range(12):
                held = jnp.where(block_of == b, rows, EMPTY)
                peak = jnp.max(jnp.max(held, axis=0), axis=0, keepdims=True)
                mass = jnp.sum(jnp.sum(jnp.exp2(held - peak), axis=0), axis=0, keepdims=True)
                found[b : b + 1, cols] = peak + jnp.log2(mass)
        new_pot = 0.5 * (pot[...] + norm[...] - LN2 * found[...])
        pot[...] = new_pot
        if step < ITERS - 1:
            spread_sent(*level_copies(turn))
            level[0:12] = LOG2E * (new_pot[0:12] + weight[...] - norm[0:12])
            spread_start(*level_copies(1 - turn))

    def combine_at(side, step, turn):
        def before(i):
            @pl.when(jnp.logical_and(k == side, i == turn))
            def _():
                combine(step)

        return before

    take_levels(1, 0)
    sums_of(0, 0, 0)
    take_levels(0, 0)
    sums_of(1, 0, 1, before=combine_at(0, 0, z // 2))
    parts_sent(1, 0)
    sums_of(1, 1, 0, staged=True, before=combine_at(1, 0, pc.own_slot // 2))
    parts_sent(0, 0)
    sums_of(0, 1, 1, staged=True, before=combine_at(1, 1, LATE))

    @pl.when(k == 0)
    def _():
        combine(1)

    take_levels(1, 2)
    parts_sent(0, 1)
    sums_of(0, 2, 0)
    take_levels(0, 2)
    parts_sent(1, 1)
    sums_of(1, 2, 1)
    combine(2)
    parts_sent(0, 2)
    parts_sent(1, 2)
    spread_sent(*level_copies(0))
    pot_out[...] = pot[0:12]


def per_device(embeds, log_weights, listing):
    emb = embeds[0]
    pairs = listing[0]
    DMA = pltpu.SemaphoreType.DMA
    any_spec = pl.BlockSpec(memory_space=pl.ANY)
    vmem = pl.BlockSpec(memory_space=pltpu.VMEM)
    f32 = jnp.float32
    pot = pl.pallas_call(
        sinkhorn_kernel,
        out_shape=jax.ShapeDtypeStruct((12, 256), f32),
        in_specs=[any_spec, vmem, any_spec],
        out_specs=vmem,
        scratch_shapes=[
            pltpu.VMEM((8, 12, 256, 256), jnp.bfloat16),
            pltpu.VMEM((8, 12, 256, 256), jnp.bfloat16),
            pltpu.VMEM((16, 8, 128), jnp.int32),
            pltpu.VMEM((12, 256), f32),
            pltpu.VMEM((12, 256, 256), jnp.bfloat16),
            pltpu.VMEM((16, 256), f32),
            pltpu.VMEM((2, 16, 16, 256), f32),
            pltpu.VMEM((16, 256), f32),
            pltpu.VMEM((8, 8, 128), jnp.int32),
            pltpu.SMEM((8, 8, 128), jnp.int32),
            pltpu.VMEM((2, 256, 128), f32),
            pltpu.VMEM((2, 256, 16), f32),
            pltpu.VMEM((16, 8, 256), f32),
            pltpu.VMEM((2, 16, 8, 256), f32),
            pltpu.VMEM((16, 256), f32),
            pltpu.VMEM((16, 256), f32),
            DMA,
            DMA,
            DMA,
            DMA,
            DMA((2,)),
            DMA((2, 2, 2)),
            DMA((2, 2, 2)),
            DMA((2, 2, 2)),
            DMA((2, 4, 2)),
            DMA((2, 4, 2)),
            DMA((2, 4, 2)),
            DMA((2, 4, 2)),
            DMA((2, 2, 2)),
            DMA((2, 2, 2)),
            DMA((2, 2, 2, 2)),
            DMA((2, 2, 2, 2)),
            DMA((2, 2, 2)),
            DMA((2, 2, 2)),
            DMA((16,)),
            DMA((8,)),
            DMA((2, 16)),
            DMA((2, 16)),
            DMA((2, 16)),
            DMA((2, 16)),
        ],
        compiler_params=pltpu.CompilerParams(collective_id=0, has_side_effects=True, vmem_limit_bytes=VMEM_CAP),
        name="sinkhorn",
    )(emb, pairs, log_weights[0])
    return pot[None]


def solution(mesh):
    placed = (
        P("side", ("group", "dev"), None, None),
        P("side", ("group", "dev"), None),
        P("side", ("group", "dev"), None),
    )
    return jax.shard_map(
        per_device,
        mesh=mesh,
        in_specs=placed,
        out_specs=P("side", ("group", "dev"), None),
        check_vma=False,
    )
```

```python
import math

import jax
import jax.numpy as jnp
from jax import lax
from jax.experimental import pallas as pl
from jax.experimental.pallas import tpu as pltpu
from jax.sharding import PartitionSpec as P

MESH = pl.DeviceIdType.MESH
ITERS = 3
LATE = 3
NX, NY, NZ = 4, 4, 8
LOG2E = math.log2(math.e)
LN2 = math.log(2.0)
INV_BLUR = 10.0
SCALE = 2.0 * INV_BLUR * LOG2E
EMPTY = -1e30
VMEM_CAP = 50 * 1024 * 1024


def where(pred, a, b):
    return jnp.where(pred, a, b)


class Place:
    def __init__(self):
        self.k = lax.axis_index("side")
        self.x = lax.axis_index("group")
        dev = lax.axis_index("dev")
        self.y = dev // NZ
        self.z = dev % NZ
        self.kq = (self.x + self.y) % 2
        self.own_slot = self.y * 2 + self.x // 2

    def dev(self, k, x, y, z):
        return (k, x, y * NZ + z)

    def source_owner(self, a):
        return self.dev(jnp.int32(0), self.x, self.y, a), jnp.logical_and(self.k == 0, self.z == a)

    def target_owner(self, d):
        y0 = d // 2
        x0 = 2 * (d % 2) + (y0 + self.k) % 2
        me = jnp.logical_and(self.k == 1, jnp.logical_and(self.x == x0, self.y == y0))
        return self.dev(jnp.int32(1), x0, y0, self.z), me

    def owner(self, j):
        return self.source_owner(jnp.int32(j)) if j < 8 else self.target_owner(jnp.int32(j - 8))

    def meeter(self, j):
        src = self.k == 0
        kk = where(src, j % 2, self.kq)
        xx = where(src, self.x, j % 4)
        yy = where(src, self.y, j // 4)
        zz = where(src, j // 2, self.z)
        me = jnp.logical_and(
            jnp.logical_and(kk == self.k, xx == self.x), jnp.logical_and(yy == self.y, zz == self.z)
        )
        return self.dev(kk, xx, yy, zz), me

    def peers(self):
        return 16 - where(jnp.logical_or(self.k == 0, self.kq == 1), 1, 0)

    def level_slot(self):
        return where(self.k == 0, self.z, 8 + self.own_slot)

    def meet_slot(self, side):
        return self.z * 2 + self.k if side == 0 else self.y * 4 + self.x


def remote(src, dst, send_sem, recv_sem, device):
    return pltpu.make_async_remote_copy(
        src_ref=src, dst_ref=dst, send_sem=send_sem, recv_sem=recv_sem, device_id=device, device_id_type=MESH
    )


def spread_start(pc, level, table, send_sem, recv_sem):
    slot = pc.level_slot()
    for j in range(16):
        device, me = pc.meeter(j)

        @pl.when(jnp.logical_not(me))
        def _():
            remote(level, table.at[slot], send_sem.at[j], recv_sem.at[slot], device).start()

        @pl.when(me)
        def _():
            table[slot] = level[...]


def spread_landed(pc, level, table, send_sem, recv_sem, side):
    for j in range(8 * side, 8 * side + 8):
        owner, mine = pc.owner(j)

        @pl.when(jnp.logical_not(mine))
        def _():
            remote(level, table.at[j], send_sem.at[j], recv_sem.at[j], owner).wait_recv()


def spread_sent(pc, level, table, send_sem, recv_sem):
    for j in range(16):
        device, me = pc.meeter(j)

        @pl.when(jnp.logical_not(me))
        def _():
            remote(level, table.at[j], send_sem.at[j], recv_sem.at[j], device).wait_send()


def signal(sem, device):
    pl.semaphore_signal(sem, inc=1, device_id=device, device_id_type=MESH)


def sinkhorn_kernel(
    emb, pairs, weights, pot_out,
    src, tgt, meet, weight, mine_blocks, norm, table, level, plan, todo, turned, turned_one, parts, gathered, pot, found,
    todo_sem, norm_sem, weight_sem, local_sem, own_sem, z_out, first_out, next_out, z_send, z_recv, sib_send, sib_recv,
    first_send, first_recv, next_send, next_recv, relay_send, relay_recv,
    plan_send, plan_recv, lv_send, lv_recv, part_send, part_recv,
):
    pc = Place()
    k, x, y, z = pc.k, pc.x, pc.y, pc.z
    sibling = pc.dev(1 - k, x, y, z)
    zdev = [pc.dev(k, x, y, (z + 1) % NZ), pc.dev(k, x, y, (z + NZ - 1) % NZ)]
    xdev = [pc.dev(k, (x + 1) % NX, y, z), pc.dev(k, (x + NX - 1) % NX, y, z)]
    ydev = [pc.dev(k, x, (y + 1) % NY, z), pc.dev(k, x, (y + NY - 1) % NY, z)]

    barrier = pltpu.get_barrier_semaphore()
    for device in [sibling] + zdev + xdev + ydev:
        signal(barrier, device)
    for j in range(16):
        device, mine = pc.owner(j)

        @pl.when(jnp.logical_not(mine))
        def _():
            signal(barrier, device)

    pl.semaphore_wait(barrier, 7 + pc.peers())

    native = k == pc.kq

    def src_at(h, z0, s):
        return src.at[z0, pl.ds(6 * h + 3 * s, 3)]

    def tgt_at(f, line, o, s, core=k):
        if f == 0:
            return tgt.at[line * 2 + o, pl.ds(3 * s, 3)]
        return tgt.at[(2 * o + (line + core) % 2) * 2 + line // 2, pl.ds(6 + 3 * s, 3)]

    line_of = [y, x]
    spot_of = [x, y]
    spread_dev = [xdev, ydev]
    onward_dev = [ydev, xdev]

    own_line = pc.own_slot

    def z_first(way, h, s):
        part = emb.at[pl.ds(6 * h + 3 * s, 3)]
        z1 = (z + 1) % NZ if way == 0 else (z + NZ - 1) % NZ
        return remote(
            part, src_at(h, z, s), z_out.at[way, h, s], z_recv.at[way, 0, s], pc.dev(jnp.int32(h), x, y, z1)
        )

    def to_core(device):
        return (pc.kq,) + device[1:]

    def tgt_first(f, way, s):
        part = emb.at[pl.ds(6 * f + 3 * s, 3)]
        home_at = tgt.at[own_line, pl.ds(6 * f + 3 * s, 3)]
        return remote(part, home_at, first_out.at[f, way, s], first_recv.at[f, way, s], to_core(spread_dev[f][way]))

    def tgt_next(f, way, s):
        part = emb.at[pl.ds(6 * f + 3 * s, 3)]
        home_at = tgt.at[own_line, pl.ds(6 * f + 3 * s, 3)]
        return remote(
            part, home_at, next_out.at[f, way, s], next_recv.at[f, way, spot_of[f] // 2, s], to_core(onward_dev[f][way])
        )

    def norm_copy():
        return pltpu.make_async_copy(emb, mine_blocks, norm_sem)

    def src_local():
        return pltpu.make_async_copy(emb, src.at[z], local_sem)

    def src_sibling():
        return remote(emb, src.at[z], own_sem.at[0], own_sem.at[1], sibling)

    def tgt_local():
        return pltpu.make_async_copy(emb, tgt.at[own_line], local_sem)

    def tgt_sibling():
        return remote(emb, tgt.at[own_line], own_sem.at[0], own_sem.at[1], sibling)

    @pl.when(k == 0)
    def _():
        for s in range(2):
            for way in range(2):
                for h in range(2):
                    z_first(way, h, s).start()
        src_local().start()
        src_sibling().start()

    @pl.when(k == 1)
    def _():
        for s in range(2):
            for f in range(2):
                for way in range(2):
                    tgt_first(f, way, s).start()
        for s in range(2):
            for f in range(2):
                for way in range(2):
                    tgt_next(f, way, s).start()

        @pl.when(pc.kq == 1)
        def _():
            tgt_local().start()

        @pl.when(pc.kq == 0)
        def _():
            tgt_sibling().start()

    norm_copy().start()
    weight_copy = pltpu.make_async_copy(weights, weight, weight_sem)
    weight_copy.start()

    own_local = pairs[:, 0:1] - 12 * (x * 32 + y * 8 + z)
    far = pairs[:, 1:2]
    far_dev = (far * 43691) >> 19
    far_local = far - 12 * far_dev
    fx = far_dev >> 5
    fy = (far_dev >> 3) & 3
    fz = far_dev & 7
    place_src = (fz * 2 + ((fx + fy) & 1)) * 8 + fy * 2 + (fx >> 1)
    place_tgt = (fy * 4 + fx) * 8 + fz
    place = jnp.where(k == 0, place_src, place_tgt)
    hot = place == lax.broadcasted_iota(jnp.int32, (60, 128), 1)
    line = jnp.sum(jnp.where(hot, own_local * 16 + far_local + 1, 0), axis=0, keepdims=True)
    meet[...] = jnp.broadcast_to(line, (128, 128)).T.reshape(16, 8, 128)
    weight_copy.wait()
    norm_copy().wait()
    ones = jnp.ones((8, 256), jnp.bfloat16)
    norm[...] = jnp.zeros(norm.shape, jnp.float32)
    level[...] = jnp.zeros(level.shape, jnp.float32)

    def norm_of(b, carry):
        value = mine_blocks[b].astype(jnp.float32)
        square = value * value
        high = square.astype(jnp.bfloat16)
        low = (square - high.astype(jnp.float32)).astype(jnp.bfloat16)
        across = (((1,), (1,)), ((), ()))
        total = lax.dot_general(ones, high, across, preferred_element_type=jnp.float32)
        total = total + lax.dot_general(ones, low, across, preferred_element_type=jnp.float32)
        norm[pl.ds(b, 1), :] = INV_BLUR * total[0:1]
        return carry

    lax.fori_loop(0, 12, norm_of, 0)
    level[0:12] = LOG2E * (weight[...] - norm[0:12])
    spread_start(pc, level, table.at[0], lv_send.at[0], lv_recv.at[0])

    def plan_copy(j, slot, device):
        return remote(meet.at[j], plan.at[slot], plan_send.at[j], plan_recv.at[slot], device)

    @pl.when(k == 0)
    def _():
        for j in range(16):
            device, me = pc.meeter(j)

            @pl.when(jnp.logical_not(me))
            def _():
                plan_copy(j, z, device).start()

            @pl.when(me)
            def _():
                plan[z] = meet[j]

    def z_copy(way, r, s):
        z0 = (z - r + NZ) % NZ if way == 0 else (z + r) % NZ
        part = src.at[z0, pl.ds(6 * k + 3 * s, 3)]
        return remote(part, part, z_send.at[way, r, s], z_recv.at[way, r, s], zdev[way])

    def z_landed(way, r, s):
        z0 = (z - r - 1 + NZ) % NZ if way == 0 else (z + r + 1) % NZ
        part = src.at[z0, pl.ds(6 * k + 3 * s, 3)]
        return remote(part, part, z_send.at[way, r, s], z_recv.at[way, r, s], zdev[way])

    def sib_copy(way, r, s):
        z0 = (z - r - 1 + NZ) % NZ if way == 0 else (z + r + 1) % NZ
        part = src.at[z0, pl.ds(6 * k + 3 * s, 3)]
        return remote(part, part, sib_send.at[way, r, s], sib_recv.at[way, r, s], sibling)

    def sib_landed(way, r, s):
        z0 = (z - r - 1 + NZ) % NZ if way == 0 else (z + r + 1) % NZ
        part = src.at[z0, pl.ds(6 * (1 - k) + 3 * s, 3)]
        return remote(part, part, sib_send.at[way, r, s], sib_recv.at[way, r, s], sibling)

    def z_subs(way, r):
        return (0, 1) if r < 3 else (way,)

    def first_copy(f, way, o, s):
        part = tgt_at(f, line_of[f], o, s)
        return remote(part, part, first_send.at[f, way, s], first_recv.at[f, way, s], spread_dev[f][way])

    def next_copy(f, way, o, s):
        part = tgt_at(f, line_of[f], o, s)
        return remote(part, part, next_send.at[f, way, o, s], next_recv.at[f, way, o, s], onward_dev[f][way])

    def from_line(f, way):
        n = line_of[f]
        return (n + 3) % 4 if way == 0 else (n + 1) % 4

    def next_landed(f, way, o, s):
        part = tgt_at(f, from_line(f, way), o, s)
        return remote(part, part, next_send.at[f, way, o, s], next_recv.at[f, way, o, s], onward_dev[f][way])

    def relay_copy(f, way, o):
        part = tgt_at(f, from_line(f, way), o, way)
        return remote(part, part, relay_send.at[f, way, o], relay_recv.at[f, way, o], onward_dev[f][way])

    def relay_landed(f, way, o):
        part = tgt_at(f, (line_of[f] + 2) % 4, o, way)
        return remote(part, part, relay_send.at[f, way, o], relay_recv.at[f, way, o], onward_dev[f][way])

    home = [spot_of[f] // 2 for f in range(2)]
    near = [[((spot_of[f] + 3) % 4) // 2, ((spot_of[f] + 1) % 4) // 2] for f in range(2)]

    def z_forward(r):
        for s in range(2):
            for way in range(2):
                if s in z_subs(way, r):
                    z_landed(way, r, s).wait_recv()
                    if r < 3 and s in z_subs(way, r + 1):
                        z_copy(way, r + 1, s).start()
                    sib_copy(way, r, s).start()

    z_forward(0)

    @pl.when(jnp.logical_not(native))
    def _():
        for s in range(2):
            for f in range(2):
                for way in range(2):
                    o = near[f][way]
                    first_copy(f, way, o, s).wait_recv()
                    if s == way:
                        first_copy(f, way, o, s).start()
                    for w in range(2):
                        next_copy(f, w, o, s).start()

    z_forward(1)

    @pl.when(native)
    def _():
        for f in range(2):
            for way in range(2):
                o = 1 - home[f]
                first_copy(f, way, o, way).wait_recv()
                for w in range(2):
                    next_copy(f, w, o, way).start()

    def onward(nth):
        for s in range(2):
            for f in range(2):
                o = home[f] if nth == 0 else 1 - home[f]
                for way in range(2):
                    next_landed(f, way, o, s).wait_recv()
                    if s == way:
                        relay_copy(f, way, o).start()

    onward(0)
    z_forward(2)

    for j in range(8):
        device, mine = pc.owner(j)

        @pl.when(jnp.logical_not(mine))
        def _():
            plan_copy(0, j, device).wait_recv()

    listed = pltpu.make_async_copy(plan, todo, todo_sem)
    listed.start()
    listed.wait()

    @pl.when(k == 0)
    def _():
        for j in range(16):
            device, me = pc.meeter(j)

            @pl.when(jnp.logical_not(me))
            def _():
                plan_copy(j, z, device).wait_send()

    for side in range(2):
        spread_landed(pc, level, table.at[0], lv_send.at[0], lv_recv.at[0], side)
        turned[side] = table[0, 8 * side : 8 * side + 8].reshape(128, 256).T
    pot[...] = jnp.zeros(pot.shape, jnp.float32)
    found[...] = jnp.zeros(found.shape, jnp.float32)

    onward(1)
    z_forward(3)

    for f in range(2):
        for way in range(2):
            for o in range(2):
                relay_landed(f, way, o).wait_recv()
    for r in range(4):
        for way in range(2):
            for s in z_subs(way, r):
                sib_landed(way, r, s).wait_recv()

    @pl.when(k == 0)
    def _():
        src_local().wait()
        src_sibling().wait_send()
        for s in range(2):
            for way in range(2):
                for h in range(2):
                    z_first(way, h, s).wait_send()

        @pl.when(pc.kq == 0)
        def _():
            tgt_sibling().wait_recv()

    @pl.when(k == 1)
    def _():
        src_sibling().wait_recv()

        @pl.when(pc.kq == 1)
        def _():
            tgt_local().wait()

        @pl.when(pc.kq == 0)
        def _():
            tgt_sibling().wait_send()

        for s in range(2):
            for f in range(2):
                for way in range(2):
                    tgt_first(f, way, s).wait_send()
                    tgt_next(f, way, s).wait_send()

    lane = lax.broadcasted_iota(jnp.int32, (256, 128), 1)
    contract = (((1,), (1,)), ((), ()))

    lane16 = lax.broadcasted_iota(jnp.int32, (256, 16), 1)

    def log_sums(a, b, bias):
        score = lax.dot_general(a, b, contract, preferred_element_type=jnp.float32) * SCALE + bias
        peak = jnp.max(score, axis=0, keepdims=True)
        return peak + jnp.log2(jnp.sum(jnp.exp2(score - peak), axis=0, keepdims=True))

    def level_copies(turn):
        return (pc, level, table.at[turn], lv_send.at[turn], lv_recv.at[turn])

    def take_levels(side, step):
        spread_landed(*level_copies(step % 2), side)
        turned[side] = table[step % 2, 8 * side : 8 * side + 8].reshape(128, 256).T

    def part_copy(side, step, i, slot, device):
        turn = step % 2
        return remote(
            parts.at[8 * side + i], gathered.at[turn, slot], part_send.at[turn, 8 * side + i], part_recv.at[turn, slot],
            device,
        )

    def part_out(side, step, i):
        device, mine = pc.source_owner(i) if side == 0 else pc.target_owner(i)
        slot = pc.meet_slot(side)

        @pl.when(jnp.logical_not(mine))
        def _():
            part_copy(side, step, i, slot, device).start()

        @pl.when(mine)
        def _():
            gathered[step % 2, slot] = parts[8 * side + i]

    def sums_of(side, step, outer, staged=False, before=None):
        def body(pair, carry):
            if before is not None:
                before(pair)
            if staged:
                for w in range(2):
                    i = pair * 2 + w
                    owner, mine = pc.source_owner(i) if outer == 0 else pc.target_owner(i)
                    _, _, rows, sent, landed = level_copies(step % 2)
                    j = 8 * outer + i

                    @pl.when(jnp.logical_not(mine))
                    def _():
                        remote(level, rows.at[j], sent.at[j], landed.at[j], owner).wait_recv()

                for w in range(2):
                    turned_one[w] = table[step % 2, 8 * outer + pair * 2 + w].T
            sums = []
            for w in range(2):
                i = pair * 2 + w
                for u in range(8):
                    a, d = (i, u) if outer == 0 else (u, i)
                    code = jnp.maximum(todo[a, d, 0] - 1, 0)
                    bs = code // 16
                    bt = code % 16
                    xs = src[a, bs]
                    ys = tgt[d, bt]
                    if side == 0:
                        left, right, row, base = ys, xs, bt, d
                    else:
                        left, right, row, base = xs, ys, bs, a
                    if staged:
                        bias = jnp.sum(jnp.where(lane16 == row, turned_one[w], 0.0), axis=1, keepdims=True)
                    else:
                        bias = jnp.sum(jnp.where(lane == base * 16 + row, turned[1 - side], 0.0), axis=1, keepdims=True)
                    sums.append(log_sums(left, right, bias))
            for w in range(2):
                i = pair * 2 + w
                for u in range(8):
                    if outer == side:
                        parts[8 * side + i, u : u + 1, :] = sums[8 * w + u]
                    else:
                        parts[8 * side + u, pl.ds(i, 1), :] = sums[8 * w + u]
            if outer == side:
                for w in range(2):
                    part_out(side, step, pair * 2 + w)
            return carry

        lax.fori_loop(0, 4, body, 0)
        if outer != side:
            for i in range(8):
                part_out(side, step, jnp.int32(i))

    def parts_sent(side, step):
        for j in range(8):
            device, mine = pc.owner(8 * side + j)

            @pl.when(jnp.logical_not(mine))
            def _():
                part_copy(side, step, j, 0, device).wait_send()

    def combine(step):
        turn = step % 2
        for j in range(16):
            device, me = pc.meeter(j)

            @pl.when(jnp.logical_not(me))
            def _():
                part_copy(0, step, 0, j, device).wait_recv()

        block_of = (meet[...] + 15) // 16 - 1
        for half in range(2):
            cols = pl.ds(128 * half, 128)
            rows = gathered[turn, :, :, cols]
            for b in range(12):
                held = jnp.where(block_of == b, rows, EMPTY)
                peak = jnp.max(jnp.max(held, axis=0), axis=0, keepdims=True)
                mass = jnp.sum(jnp.sum(jnp.exp2(held - peak), axis=0), axis=0, keepdims=True)
                found[b : b + 1, cols] = peak + jnp.log2(mass)
        new_pot = 0.5 * (pot[...] + norm[...] - LN2 * found[...])
        pot[...] = new_pot
        if step < ITERS - 1:
            spread_sent(*level_copies(turn))
            level[0:12] = LOG2E * (new_pot[0:12] + weight[...] - norm[0:12])
            spread_start(*level_copies(1 - turn))

    def combine_at(side, step, turn):
        def before(i):
            @pl.when(jnp.logical_and(k == side, i == turn))
            def _():
                combine(step)

        return before

    sums_of(0, 0, 0)
    sums_of(1, 0, 1, before=combine_at(0, 0, z // 2))
    parts_sent(1, 0)
    sums_of(1, 1, 0, staged=True, before=combine_at(1, 0, pc.own_slot // 2))
    parts_sent(0, 0)
    sums_of(0, 1, 1, staged=True, before=combine_at(1, 1, LATE))

    @pl.when(k == 0)
    def _():
        combine(1)

    take_levels(1, 2)
    parts_sent(0, 1)
    sums_of(0, 2, 0)
    take_levels(0, 2)
    parts_sent(1, 1)
    sums_of(1, 2, 1)
    combine(2)
    parts_sent(0, 2)
    parts_sent(1, 2)
    spread_sent(*level_copies(0))
    for r in range(4):
        for way in range(2):
            for s in z_subs(way, r):
                if r > 0:
                    z_copy(way, r, s).wait_send()
                sib_copy(way, r, s).wait_send()
    for f in range(2):
        for way in range(2):
            for o in range(2):
                relay_copy(f, way, o).wait_send()

            @pl.when(native)
            def _():
                next_copy(f, way, 1 - home[f], 0).wait_send()
                next_copy(f, way, 1 - home[f], 1).wait_send()

            @pl.when(jnp.logical_not(native))
            def _():
                first_copy(f, way, near[f][way], way).wait_send()
                for o in range(2):
                    for s in range(2):
                        next_copy(f, way, o, s).wait_send()

    pot_out[...] = pot[0:12]


def per_device(embeds, log_weights, listing):
    emb = embeds[0]
    pairs = listing[0]
    DMA = pltpu.SemaphoreType.DMA
    any_spec = pl.BlockSpec(memory_space=pl.ANY)
    vmem = pl.BlockSpec(memory_space=pltpu.VMEM)
    f32 = jnp.float32
    pot = pl.pallas_call(
        sinkhorn_kernel,
        out_shape=jax.ShapeDtypeStruct((12, 256), f32),
        in_specs=[any_spec, vmem, any_spec],
        out_specs=vmem,
        scratch_shapes=[
            pltpu.VMEM((8, 12, 256, 256), jnp.bfloat16),
            pltpu.VMEM((8, 12, 256, 256), jnp.bfloat16),
            pltpu.VMEM((16, 8, 128), jnp.int32),
            pltpu.VMEM((12, 256), f32),
            pltpu.VMEM((12, 256, 256), jnp.bfloat16),
            pltpu.VMEM((16, 256), f32),
            pltpu.VMEM((2, 16, 16, 256), f32),
            pltpu.VMEM((16, 256), f32),
            pltpu.VMEM((8, 8, 128), jnp.int32),
            pltpu.SMEM((8, 8, 128), jnp.int32),
            pltpu.VMEM((2, 256, 128), f32),
            pltpu.VMEM((2, 256, 16), f32),
            pltpu.VMEM((16, 8, 256), f32),
            pltpu.VMEM((2, 16, 8, 256), f32),
            pltpu.VMEM((16, 256), f32),
            pltpu.VMEM((16, 256), f32),
            DMA,
            DMA,
            DMA,
            DMA,
            DMA((2,)),
            DMA((2, 2, 2)),
            DMA((2, 2, 2)),
            DMA((2, 2, 2)),
            DMA((2, 4, 2)),
            DMA((2, 4, 2)),
            DMA((2, 4, 2)),
            DMA((2, 4, 2)),
            DMA((2, 2, 2)),
            DMA((2, 2, 2)),
            DMA((2, 2, 2, 2)),
            DMA((2, 2, 2, 2)),
            DMA((2, 2, 2)),
            DMA((2, 2, 2)),
            DMA((16,)),
            DMA((8,)),
            DMA((2, 16)),
            DMA((2, 16)),
            DMA((2, 16)),
            DMA((2, 16)),
        ],
        compiler_params=pltpu.CompilerParams(collective_id=0, has_side_effects=True, vmem_limit_bytes=VMEM_CAP),
        name="sinkhorn",
    )(emb, pairs, log_weights[0])
    return pot[None]


def solution(mesh):
    placed = (
        P("side", ("group", "dev"), None, None),
        P("side", ("group", "dev"), None),
        P("side", ("group", "dev"), None),
    )
    return jax.shard_map(
        per_device,
        mesh=mesh,
        in_specs=placed,
        out_specs=P("side", ("group", "dev"), None),
        check_vma=False,
    )
```

```python
import math

import jax
import jax.numpy as jnp
from jax import lax
from jax.experimental import pallas as pl
from jax.experimental.pallas import tpu as pltpu
from jax.sharding import PartitionSpec as P

MESH = pl.DeviceIdType.MESH
ITERS = 3
LATE = 3
NX, NY, NZ = 4, 4, 8
LOG2E = math.log2(math.e)
LN2 = math.log(2.0)
INV_BLUR = 10.0
SCALE = 2.0 * INV_BLUR * LOG2E
EMPTY = -1e30
VMEM_CAP = 50 * 1024 * 1024


def where(pred, a, b):
    return jnp.where(pred, a, b)


class Place:
    def __init__(self):
        self.k = lax.axis_index("side")
        self.x = lax.axis_index("group")
        dev = lax.axis_index("dev")
        self.y = dev // NZ
        self.z = dev % NZ
        self.kq = (self.x + self.y) % 2
        self.own_slot = self.y * 2 + self.x // 2

    def dev(self, k, x, y, z):
        return (k, x, y * NZ + z)

    def source_owner(self, a):
        return self.dev(jnp.int32(0), self.x, self.y, a), jnp.logical_and(self.k == 0, self.z == a)

    def target_owner(self, d):
        y0 = d // 2
        x0 = 2 * (d % 2) + (y0 + self.k) % 2
        me = jnp.logical_and(self.k == 1, jnp.logical_and(self.x == x0, self.y == y0))
        return self.dev(jnp.int32(1), x0, y0, self.z), me

    def owner(self, j):
        return self.source_owner(jnp.int32(j)) if j < 8 else self.target_owner(jnp.int32(j - 8))

    def meeter(self, j):
        src = self.k == 0
        kk = where(src, j % 2, self.kq)
        xx = where(src, self.x, j % 4)
        yy = where(src, self.y, j // 4)
        zz = where(src, j // 2, self.z)
        me = jnp.logical_and(
            jnp.logical_and(kk == self.k, xx == self.x), jnp.logical_and(yy == self.y, zz == self.z)
        )
        return self.dev(kk, xx, yy, zz), me

    def peers(self):
        return 16 - where(jnp.logical_or(self.k == 0, self.kq == 1), 1, 0)

    def level_slot(self):
        return where(self.k == 0, self.z, 8 + self.own_slot)

    def meet_slot(self, side):
        return self.z * 2 + self.k if side == 0 else self.y * 4 + self.x


def remote(src, dst, send_sem, recv_sem, device):
    return pltpu.make_async_remote_copy(
        src_ref=src, dst_ref=dst, send_sem=send_sem, recv_sem=recv_sem, device_id=device, device_id_type=MESH
    )


def spread_start(pc, level, table, send_sem, recv_sem):
    slot = pc.level_slot()
    for j in range(16):
        device, me = pc.meeter(j)

        @pl.when(jnp.logical_not(me))
        def _():
            remote(level, table.at[slot], send_sem.at[j], recv_sem.at[slot], device).start()

        @pl.when(me)
        def _():
            table[slot] = level[...]


def spread_landed(pc, level, table, send_sem, recv_sem, side):
    for j in range(8 * side, 8 * side + 8):
        owner, mine = pc.owner(j)

        @pl.when(jnp.logical_not(mine))
        def _():
            remote(level, table.at[j], send_sem.at[j], recv_sem.at[j], owner).wait_recv()


def spread_sent(pc, level, table, send_sem, recv_sem):
    for j in range(16):
        device, me = pc.meeter(j)

        @pl.when(jnp.logical_not(me))
        def _():
            remote(level, table.at[j], send_sem.at[j], recv_sem.at[j], device).wait_send()


def signal(sem, device):
    pl.semaphore_signal(sem, inc=1, device_id=device, device_id_type=MESH)


def sinkhorn_kernel(
    emb, pairs, weights, pot_out,
    src, tgt, meet, weight, mine_blocks, norm, table, level, plan, todo, turned, turned_one, parts, gathered, pot, found,
    todo_sem, norm_sem, weight_sem, local_sem, own_sem, z_out, first_out, next_out, z_send, z_recv, sib_send, sib_recv,
    first_send, first_recv, next_send, next_recv, relay_send, relay_recv,
    plan_send, plan_recv, lv_send, lv_recv, part_send, part_recv,
):
    pc = Place()
    k, x, y, z = pc.k, pc.x, pc.y, pc.z
    sibling = pc.dev(1 - k, x, y, z)
    zdev = [pc.dev(k, x, y, (z + 1) % NZ), pc.dev(k, x, y, (z + NZ - 1) % NZ)]
    xdev = [pc.dev(k, (x + 1) % NX, y, z), pc.dev(k, (x + NX - 1) % NX, y, z)]
    ydev = [pc.dev(k, x, (y + 1) % NY, z), pc.dev(k, x, (y + NY - 1) % NY, z)]

    barrier = pltpu.get_barrier_semaphore()
    for device in [sibling] + zdev + xdev + ydev:
        signal(barrier, device)
    for j in range(16):
        device, mine = pc.owner(j)

        @pl.when(jnp.logical_not(mine))
        def _():
            signal(barrier, device)

    pl.semaphore_wait(barrier, 7 + pc.peers())

    native = k == pc.kq

    def src_at(h, z0, s):
        return src.at[z0, pl.ds(6 * h + 3 * s, 3)]

    def tgt_at(f, line, o, s, core=k):
        if f == 0:
            return tgt.at[line * 2 + o, pl.ds(3 * s, 3)]
        return tgt.at[(2 * o + (line + core) % 2) * 2 + line // 2, pl.ds(6 + 3 * s, 3)]

    line_of = [y, x]
    spot_of = [x, y]
    spread_dev = [xdev, ydev]
    onward_dev = [ydev, xdev]

    own_line = pc.own_slot

    def z_first(way, h, s):
        part = emb.at[pl.ds(6 * h + 3 * s, 3)]
        z1 = (z + 1) % NZ if way == 0 else (z + NZ - 1) % NZ
        return remote(
            part, src_at(h, z, s), z_out.at[way, h, s], z_recv.at[way, 0, s], pc.dev(jnp.int32(h), x, y, z1)
        )

    def to_core(device):
        return (pc.kq,) + device[1:]

    def tgt_first(f, way, s):
        part = emb.at[pl.ds(6 * f + 3 * s, 3)]
        home_at = tgt.at[own_line, pl.ds(6 * f + 3 * s, 3)]
        return remote(part, home_at, first_out.at[f, way, s], first_recv.at[f, way, s], to_core(spread_dev[f][way]))

    def tgt_next(f, way, s):
        part = emb.at[pl.ds(6 * f + 3 * s, 3)]
        home_at = tgt.at[own_line, pl.ds(6 * f + 3 * s, 3)]
        return remote(
            part, home_at, next_out.at[f, way, s], next_recv.at[f, way, spot_of[f] // 2, s], to_core(onward_dev[f][way])
        )

    def norm_copy():
        return pltpu.make_async_copy(emb, mine_blocks, norm_sem)

    def src_local():
        return pltpu.make_async_copy(emb, src.at[z], local_sem)

    def src_sibling():
        return remote(emb, src.at[z], own_sem.at[0], own_sem.at[1], sibling)

    def tgt_local():
        return pltpu.make_async_copy(emb, tgt.at[own_line], local_sem)

    def tgt_sibling():
        return remote(emb, tgt.at[own_line], own_sem.at[0], own_sem.at[1], sibling)

    @pl.when(k == 0)
    def _():
        for s in range(2):
            for way in range(2):
                for h in range(2):
                    z_first(way, h, s).start()
        src_local().start()
        src_sibling().start()

    @pl.when(k == 1)
    def _():
        for s in range(2):
            for f in range(2):
                for way in range(2):
                    tgt_first(f, way, s).start()
        for s in range(2):
            for f in range(2):
                for way in range(2):
                    tgt_next(f, way, s).start()

        @pl.when(pc.kq == 1)
        def _():
            tgt_local().start()

        @pl.when(pc.kq == 0)
        def _():
            tgt_sibling().start()

    norm_copy().start()
    weight_copy = pltpu.make_async_copy(weights, weight, weight_sem)
    weight_copy.start()

    own_local = pairs[:, 0:1] - 12 * (x * 32 + y * 8 + z)
    far = pairs[:, 1:2]
    far_dev = (far * 43691) >> 19
    far_local = far - 12 * far_dev
    fx = far_dev >> 5
    fy = (far_dev >> 3) & 3
    fz = far_dev & 7
    place_src = (fz * 2 + ((fx + fy) & 1)) * 8 + fy * 2 + (fx >> 1)
    place_tgt = (fy * 4 + fx) * 8 + fz
    place = jnp.where(k == 0, place_src, place_tgt)
    hot = place == lax.broadcasted_iota(jnp.int32, (60, 128), 1)
    line = jnp.sum(jnp.where(hot, own_local * 16 + far_local + 1, 0), axis=0, keepdims=True)
    meet[...] = jnp.broadcast_to(line, (128, 128)).T.reshape(16, 8, 128)
    weight_copy.wait()
    norm_copy().wait()
    ones = jnp.ones((8, 256), jnp.bfloat16)
    norm[...] = jnp.zeros(norm.shape, jnp.float32)
    level[...] = jnp.zeros(level.shape, jnp.float32)

    def norm_of(b, carry):
        value = mine_blocks[b].astype(jnp.float32)
        square = value * value
        high = square.astype(jnp.bfloat16)
        low = (square - high.astype(jnp.float32)).astype(jnp.bfloat16)
        across = (((1,), (1,)), ((), ()))
        total = lax.dot_general(ones, high, across, preferred_element_type=jnp.float32)
        total = total + lax.dot_general(ones, low, across, preferred_element_type=jnp.float32)
        norm[pl.ds(b, 1), :] = INV_BLUR * total[0:1]
        return carry

    lax.fori_loop(0, 12, norm_of, 0)
    level[0:12] = LOG2E * (weight[...] - norm[0:12])
    spread_start(pc, level, table.at[0], lv_send.at[0], lv_recv.at[0])

    def plan_copy(j, slot, device):
        return remote(meet.at[j], plan.at[slot], plan_send.at[j], plan_recv.at[slot], device)

    @pl.when(k == 0)
    def _():
        for j in range(16):
            device, me = pc.meeter(j)

            @pl.when(jnp.logical_not(me))
            def _():
                plan_copy(j, z, device).start()

            @pl.when(me)
            def _():
                plan[z] = meet[j]

    def z_copy(way, r, s):
        z0 = (z - r + NZ) % NZ if way == 0 else (z + r) % NZ
        part = src.at[z0, pl.ds(6 * k + 3 * s, 3)]
        return remote(part, part, z_send.at[way, r, s], z_recv.at[way, r, s], zdev[way])

    def z_landed(way, r, s):
        z0 = (z - r - 1 + NZ) % NZ if way == 0 else (z + r + 1) % NZ
        part = src.at[z0, pl.ds(6 * k + 3 * s, 3)]
        return remote(part, part, z_send.at[way, r, s], z_recv.at[way, r, s], zdev[way])

    def sib_copy(way, r, s):
        z0 = (z - r - 1 + NZ) % NZ if way == 0 else (z + r + 1) % NZ
        part = src.at[z0, pl.ds(6 * k + 3 * s, 3)]
        return remote(part, part, sib_send.at[way, r, s], sib_recv.at[way, r, s], sibling)

    def sib_landed(way, r, s):
        z0 = (z - r - 1 + NZ) % NZ if way == 0 else (z + r + 1) % NZ
        part = src.at[z0, pl.ds(6 * (1 - k) + 3 * s, 3)]
        return remote(part, part, sib_send.at[way, r, s], sib_recv.at[way, r, s], sibling)

    def z_subs(way, r):
        return (0, 1) if r < 3 else (way,)

    def first_copy(f, way, o, s):
        part = tgt_at(f, line_of[f], o, s)
        return remote(part, part, first_send.at[f, way, s], first_recv.at[f, way, s], spread_dev[f][way])

    def next_copy(f, way, o, s):
        part = tgt_at(f, line_of[f], o, s)
        return remote(part, part, next_send.at[f, way, o, s], next_recv.at[f, way, o, s], onward_dev[f][way])

    def from_line(f, way):
        n = line_of[f]
        return (n + 3) % 4 if way == 0 else (n + 1) % 4

    def next_landed(f, way, o, s):
        part = tgt_at(f, from_line(f, way), o, s)
        return remote(part, part, next_send.at[f, way, o, s], next_recv.at[f, way, o, s], onward_dev[f][way])

    def relay_copy(f, way, o):
        part = tgt_at(f, from_line(f, way), o, way)
        return remote(part, part, relay_send.at[f, way, o], relay_recv.at[f, way, o], onward_dev[f][way])

    def relay_landed(f, way, o):
        part = tgt_at(f, (line_of[f] + 2) % 4, o, way)
        return remote(part, part, relay_send.at[f, way, o], relay_recv.at[f, way, o], onward_dev[f][way])

    home = [spot_of[f] // 2 for f in range(2)]
    near = [[((spot_of[f] + 3) % 4) // 2, ((spot_of[f] + 1) % 4) // 2] for f in range(2)]

    def z_forward(r):
        for s in range(2):
            for way in range(2):
                if s in z_subs(way, r):
                    z_landed(way, r, s).wait_recv()
                    if r < 3 and s in z_subs(way, r + 1):
                        z_copy(way, r + 1, s).start()
                    sib_copy(way, r, s).start()

    z_forward(0)

    @pl.when(jnp.logical_not(native))
    def _():
        for s in range(2):
            for f in range(2):
                for way in range(2):
                    o = near[f][way]
                    first_copy(f, way, o, s).wait_recv()
                    if s == way:
                        first_copy(f, way, o, s).start()
                    for w in range(2):
                        next_copy(f, w, o, s).start()

    z_forward(1)

    @pl.when(native)
    def _():
        for f in range(2):
            for way in range(2):
                o = 1 - home[f]
                first_copy(f, way, o, way).wait_recv()
                for w in range(2):
                    next_copy(f, w, o, way).start()

    def onward(nth):
        for s in range(2):
            for f in range(2):
                o = home[f] if nth == 0 else 1 - home[f]
                for way in range(2):
                    next_landed(f, way, o, s).wait_recv()
                    if s == way:
                        relay_copy(f, way, o).start()

    onward(0)

    for j in range(8):
        device, mine = pc.owner(j)

        @pl.when(jnp.logical_not(mine))
        def _():
            plan_copy(0, j, device).wait_recv()

    listed = pltpu.make_async_copy(plan, todo, todo_sem)
    listed.start()
    listed.wait()

    @pl.when(k == 0)
    def _():
        for j in range(16):
            device, me = pc.meeter(j)

            @pl.when(jnp.logical_not(me))
            def _():
                plan_copy(j, z, device).wait_send()

    for side in range(2):
        spread_landed(pc, level, table.at[0], lv_send.at[0], lv_recv.at[0], side)
        turned[side] = table[0, 8 * side : 8 * side + 8].reshape(128, 256).T
    pot[...] = jnp.zeros(pot.shape, jnp.float32)
    found[...] = jnp.zeros(found.shape, jnp.float32)

    onward(1)
    z_forward(2)
    z_forward(3)

    for f in range(2):
        for way in range(2):
            for o in range(2):
                relay_landed(f, way, o).wait_recv()
    for r in range(4):
        for way in range(2):
            for s in z_subs(way, r):
                sib_landed(way, r, s).wait_recv()

    @pl.when(k == 0)
    def _():
        src_local().wait()
        src_sibling().wait_send()
        for s in range(2):
            for way in range(2):
                for h in range(2):
                    z_first(way, h, s).wait_send()

        @pl.when(pc.kq == 0)
        def _():
            tgt_sibling().wait_recv()

    @pl.when(k == 1)
    def _():
        src_sibling().wait_recv()

        @pl.when(pc.kq == 1)
        def _():
            tgt_local().wait()

        @pl.when(pc.kq == 0)
        def _():
            tgt_sibling().wait_send()

        for s in range(2):
            for f in range(2):
                for way in range(2):
                    tgt_first(f, way, s).wait_send()
                    tgt_next(f, way, s).wait_send()

    lane = lax.broadcasted_iota(jnp.int32, (256, 128), 1)
    contract = (((1,), (1,)), ((), ()))

    lane16 = lax.broadcasted_iota(jnp.int32, (256, 16), 1)

    def log_sums(a, b, bias):
        score = lax.dot_general(a, b, contract, preferred_element_type=jnp.float32) * SCALE + bias
        peak = jnp.max(score, axis=0, keepdims=True)
        return peak + jnp.log2(jnp.sum(jnp.exp2(score - peak), axis=0, keepdims=True))

    def level_copies(turn):
        return (pc, level, table.at[turn], lv_send.at[turn], lv_recv.at[turn])

    def take_levels(side, step):
        spread_landed(*level_copies(step % 2), side)
        turned[side] = table[step % 2, 8 * side : 8 * side + 8].reshape(128, 256).T

    def part_copy(side, step, i, slot, device):
        turn = step % 2
        return remote(
            parts.at[8 * side + i], gathered.at[turn, slot], part_send.at[turn, 8 * side + i], part_recv.at[turn, slot],
            device,
        )

    def part_out(side, step, i):
        device, mine = pc.source_owner(i) if side == 0 else pc.target_owner(i)
        slot = pc.meet_slot(side)

        @pl.when(jnp.logical_not(mine))
        def _():
            part_copy(side, step, i, slot, device).start()

        @pl.when(mine)
        def _():
            gathered[step % 2, slot] = parts[8 * side + i]

    def sums_of(side, step, outer, staged=False, before=None):
        def body(pair, carry):
            if before is not None:
                before(pair)
            if staged:
                for w in range(2):
                    i = pair * 2 + w
                    owner, mine = pc.source_owner(i) if outer == 0 else pc.target_owner(i)
                    _, _, rows, sent, landed = level_copies(step % 2)
                    j = 8 * outer + i

                    @pl.when(jnp.logical_not(mine))
                    def _():
                        remote(level, rows.at[j], sent.at[j], landed.at[j], owner).wait_recv()

                for w in range(2):
                    turned_one[w] = table[step % 2, 8 * outer + pair * 2 + w].T
            sums = []
            for w in range(2):
                i = pair * 2 + w
                for u in range(8):
                    a, d = (i, u) if outer == 0 else (u, i)
                    code = jnp.maximum(todo[a, d, 0] - 1, 0)
                    bs = code // 16
                    bt = code % 16
                    xs = src[a, bs]
                    ys = tgt[d, bt]
                    if side == 0:
                        left, right, row, base = ys, xs, bt, d
                    else:
                        left, right, row, base = xs, ys, bs, a
                    if staged:
                        bias = jnp.sum(jnp.where(lane16 == row, turned_one[w], 0.0), axis=1, keepdims=True)
                    else:
                        bias = jnp.sum(jnp.where(lane == base * 16 + row, turned[1 - side], 0.0), axis=1, keepdims=True)
                    sums.append(log_sums(left, right, bias))
            for w in range(2):
                i = pair * 2 + w
                for u in range(8):
                    if outer == side:
                        parts[8 * side + i, u : u + 1, :] = sums[8 * w + u]
                    else:
                        parts[8 * side + u, pl.ds(i, 1), :] = sums[8 * w + u]
            if outer == side:
                for w in range(2):
                    part_out(side, step, pair * 2 + w)
            return carry

        lax.fori_loop(0, 4, body, 0)
        if outer != side:
            for i in range(8):
                part_out(side, step, jnp.int32(i))

    def parts_sent(side, step):
        for j in range(8):
            device, mine = pc.owner(8 * side + j)

            @pl.when(jnp.logical_not(mine))
            def _():
                part_copy(side, step, j, 0, device).wait_send()

    def combine(step):
        turn = step % 2
        for j in range(16):
            device, me = pc.meeter(j)

            @pl.when(jnp.logical_not(me))
            def _():
                part_copy(0, step, 0, j, device).wait_recv()

        block_of = (meet[...] + 15) // 16 - 1
        for half in range(2):
            cols = pl.ds(128 * half, 128)
            rows = gathered[turn, :, :, cols]
            for b in range(12):
                held = jnp.where(block_of == b, rows, EMPTY)
                peak = jnp.max(jnp.max(held, axis=0), axis=0, keepdims=True)
                mass = jnp.sum(jnp.sum(jnp.exp2(held - peak), axis=0), axis=0, keepdims=True)
                found[b : b + 1, cols] = peak + jnp.log2(mass)
        new_pot = 0.5 * (pot[...] + norm[...] - LN2 * found[...])
        pot[...] = new_pot
        if step < ITERS - 1:
            spread_sent(*level_copies(turn))
            level[0:12] = LOG2E * (new_pot[0:12] + weight[...] - norm[0:12])
            spread_start(*level_copies(1 - turn))

    def combine_at(side, step, turn):
        def before(i):
            @pl.when(jnp.logical_and(k == side, i == turn))
            def _():
                combine(step)

        return before

    sums_of(0, 0, 0)
    sums_of(1, 0, 1, before=combine_at(0, 0, z // 2))
    parts_sent(1, 0)
    sums_of(1, 1, 0, staged=True, before=combine_at(1, 0, pc.own_slot // 2))
    parts_sent(0, 0)
    sums_of(0, 1, 1, staged=True, before=combine_at(1, 1, LATE))

    @pl.when(k == 0)
    def _():
        combine(1)

    take_levels(1, 2)
    parts_sent(0, 1)
    sums_of(0, 2, 0)
    take_levels(0, 2)
    parts_sent(1, 1)
    sums_of(1, 2, 1)
    combine(2)
    parts_sent(0, 2)
    parts_sent(1, 2)
    spread_sent(*level_copies(0))
    for r in range(4):
        for way in range(2):
            for s in z_subs(way, r):
                if r > 0:
                    z_copy(way, r, s).wait_send()
                sib_copy(way, r, s).wait_send()
    for f in range(2):
        for way in range(2):
            for o in range(2):
                relay_copy(f, way, o).wait_send()

            @pl.when(native)
            def _():
                next_copy(f, way, 1 - home[f], 0).wait_send()
                next_copy(f, way, 1 - home[f], 1).wait_send()

            @pl.when(jnp.logical_not(native))
            def _():
                first_copy(f, way, near[f][way], way).wait_send()
                for o in range(2):
                    for s in range(2):
                        next_copy(f, way, o, s).wait_send()

    pot_out[...] = pot[0:12]


def per_device(embeds, log_weights, listing):
    emb = embeds[0]
    pairs = listing[0]
    DMA = pltpu.SemaphoreType.DMA
    any_spec = pl.BlockSpec(memory_space=pl.ANY)
    vmem = pl.BlockSpec(memory_space=pltpu.VMEM)
    f32 = jnp.float32
    pot = pl.pallas_call(
        sinkhorn_kernel,
        out_shape=jax.ShapeDtypeStruct((12, 256), f32),
        in_specs=[any_spec, vmem, any_spec],
        out_specs=vmem,
        scratch_shapes=[
            pltpu.VMEM((8, 12, 256, 256), jnp.bfloat16),
            pltpu.VMEM((8, 12, 256, 256), jnp.bfloat16),
            pltpu.VMEM((16, 8, 128), jnp.int32),
            pltpu.VMEM((12, 256), f32),
            pltpu.VMEM((12, 256, 256), jnp.bfloat16),
            pltpu.VMEM((16, 256), f32),
            pltpu.VMEM((2, 16, 16, 256), f32),
            pltpu.VMEM((16, 256), f32),
            pltpu.VMEM((8, 8, 128), jnp.int32),
            pltpu.SMEM((8, 8, 128), jnp.int32),
            pltpu.VMEM((2, 256, 128), f32),
            pltpu.VMEM((2, 256, 16), f32),
            pltpu.VMEM((16, 8, 256), f32),
            pltpu.VMEM((2, 16, 8, 256), f32),
            pltpu.VMEM((16, 256), f32),
            pltpu.VMEM((16, 256), f32),
            DMA,
            DMA,
            DMA,
            DMA,
            DMA((2,)),
            DMA((2, 2, 2)),
            DMA((2, 2, 2)),
            DMA((2, 2, 2)),
            DMA((2, 4, 2)),
            DMA((2, 4, 2)),
            DMA((2, 4, 2)),
            DMA((2, 4, 2)),
            DMA((2, 2, 2)),
            DMA((2, 2, 2)),
            DMA((2, 2, 2, 2)),
            DMA((2, 2, 2, 2)),
            DMA((2, 2, 2)),
            DMA((2, 2, 2)),
            DMA((16,)),
            DMA((8,)),
            DMA((2, 16)),
            DMA((2, 16)),
            DMA((2, 16)),
            DMA((2, 16)),
        ],
        compiler_params=pltpu.CompilerParams(collective_id=0, has_side_effects=True, vmem_limit_bytes=VMEM_CAP),
        name="sinkhorn",
    )(emb, pairs, log_weights[0])
    return pot[None]


def solution(mesh):
    placed = (
        P("side", ("group", "dev"), None, None),
        P("side", ("group", "dev"), None),
        P("side", ("group", "dev"), None),
    )
    return jax.shard_map(
        per_device,
        mesh=mesh,
        in_specs=placed,
        out_specs=P("side", ("group", "dev"), None),
        check_vma=False,
    )
```
